32 devices in a mesh: section: 2 (over core), dp: 4 (over z), tensor: 4 (over y, x).
Axes of the slice: x: 2, y: 2, z: 4, core: 2. Of those that a mesh axis runs over, the one named last changes fastest.
Arguments:
- inputs: bfloat16 [2, 4096, 1024], P(None, ('dp', 'tensor')), may hold values from -6 to 6
- lengths: int32 [2, 4, 2], P(None, 'dp'), may hold values from 0 to 1024, as said below
- norm_gain: float32 [2, 2, 1024], P('section'), may hold values from 0.5 to 1.5
- w_query: bfloat16 [2, 1024, 1024], P('section', 'dp', 'tensor'), may hold values from -0.1875 to 0.1875
- w_key: bfloat16 [2, 1024, 1024], P('section', 'dp', 'tensor'), may hold values from -0.1875 to 0.1875
- w_value: bfloat16 [2, 1024, 2048], P('section', 'dp', 'tensor'), may hold values from -0.1875 to 0.1875
- w_gate: bfloat16 [2, 1024, 2048], P('section', 'dp', 'tensor'), may hold values from -0.1875 to 0.1875
- w_decay: bfloat16 [2, 1024, 16], P('section', 'dp', 'tensor'), may hold values from -0.1875 to 0.1875
- conv_weight: float32 [2, 4, 8, 512], P('section'), may hold values from -3 to 3
- head_rate: float32 [2, 8], P('section'), may hold values from -1 to 1.5
- head_bias: float32 [2, 8], P('section'), may hold values from -6 to -2
- out_gain: float32 [2, 256], P('section'), may hold values from 0.5 to 1.5
- w_out: bfloat16 [2, 2048, 1024], P('section', 'tensor', 'dp'), may hold values from -0.25 to 0.25
- w_updown: bfloat16 [2, 1024, 2, 2816], P('section', 'dp', None, 'tensor'), may hold values from -0.1875 to 0.1875
- w_down: bfloat16 [2, 2816, 1024], P('section', 'tensor', 'dp'), may hold values from -0.109375 to 0.109375
- cotangent: bfloat16 [2, 4096, 1024], P(None, ('dp', 'tensor')), may hold values from -6 to 6
Outputs:
- output: bfloat16 [2, 4096, 1024], P('section', ('dp', 'tensor'))
- input_grad: bfloat16 [2, 4096, 1024], P('section', ('dp', 'tensor'))
- grad_norm_gain: float32 [2, 2, 1024], P('section')
- grad_query: float32 [2, 1024, 1024], P('section', 'dp', 'tensor')
- grad_key: float32 [2, 1024, 1024], P('section', 'dp', 'tensor')
- grad_value: float32 [2, 1024, 2048], P('section', 'dp', 'tensor')
- grad_gate: float32 [2, 1024, 2048], P('section', 'dp', 'tensor')
- grad_decay: float32 [2, 1024, 16], P('section', 'dp', 'tensor')
- grad_conv: float32 [2, 4, 8, 512], P('section')
- grad_rate: float32 [2, 8], P('section')
- grad_bias: float32 [2, 8], P('section')
- grad_out_gain: float32 [2, 256], P('section')
- grad_out: float32 [2, 2048, 1024], P('section', 'tensor', 'dp')
- grad_updown: float32 [2, 1024, 2, 2816], P('section', 'dp', None, 'tensor')
- grad_down: float32 [2, 2816, 1024], P('section', 'tensor', 'dp')
The draws below stay inside these ranges and needn't reach their ends.
Inputs may be any that keep to these rules, and one draw needn't show every extreme that they name: Each buffer's sequences lie back to back from its first token in slot order; lengths are multiples of 64 and a buffer's sum is at most 1024; the first slot holds 512 tokens or more; a zero length is an empty slot; for each dp index one micro-batch's buffer is one sequence of 1024 tokens.
All inputs are finite; a program needn't handle non-finite values.
Results may differ from the reference program's by a relative error of at most 0.025.
Values may be sent and summed in bfloat16 or wider, within the bound.
No kernel may reach another device: no remote copies, remote signals or barrier semaphores. Data moves between devices by JAX's collectives and lax.ppermute only.
A program may use at most 448 MiB of HBM per device.

```python
import jax
import jax.numpy as jnp
from jax import lax

D = 1024
HEADS = 8
KEYS = 128
VALS = 256
FF = 2816
CONV = 4
BLOCK = 64
BUF = 1024
MICRO = 2
SLOTS = 2
LAYERS = 2
TOKENS = 4096
N_DP = 4


def draw_lengths(key, part):
    key = jax.random.fold_in(key, 7)
    first_key, second_key, pick_key = jax.random.split(key, 3)
    blocks = BUF // BLOCK
    first = jax.random.randint(first_key, (MICRO, N_DP), blocks // 2, blocks + 1)
    chosen = jax.random.randint(pick_key, (N_DP,), 0, MICRO)
    whole = jnp.arange(MICRO, dtype=jnp.int32)[:, None] == chosen[None, :]
    first = jnp.where(whole, blocks, first)
    second = jax.random.randint(second_key, (MICRO, N_DP), 0, blocks + 1) % (blocks - first + 1)
    return (BLOCK * jnp.stack([first, second], axis=-1)).astype(jnp.int32)


def block_scale(key, shape, cuts, smallest, top_value):
    loudness, own = 1.0, jax.random.fold_in(key, 6)
    for dim, parts in cuts:
        steps = jnp.exp(jax.random.uniform(jax.random.fold_in(own, dim), (parts,), jnp.float32, smallest / len(cuts), top_value / len(cuts)))
        loudness = loudness * jnp.repeat(steps, shape[dim] // parts).reshape([-1 if axis == dim else 1 for axis in range(len(shape))])
    return loudness


def normal_values(stream_key, extent, width, most, cuts=(), held_as=jnp.bfloat16):
    level = block_scale(stream_key, extent, cuts, -0.22, 0.18) if cuts else 1.0
    entries = jax.random.normal(stream_key, extent, jnp.float32) * width * level
    return jnp.minimum(jnp.maximum(entries, -most), most).astype(held_as)


def setup_inputs(seed: int = 0) -> dict:
    streams_of = jax.random.split(jax.random.key(seed), 17)
    return {
        "inputs": normal_values(streams_of[0], (MICRO, TOKENS, D), 1.0, 6.0, ((1, 16),)),
        "lengths": draw_lengths(jax.random.fold_in(streams_of[16], 71), 0),
        "norm_gain": jnp.clip(1.0 + 0.1 * jax.random.normal(streams_of[2], (LAYERS, 2, D), jnp.float32), 0.5, 1.5),
        "w_query": normal_values(streams_of[3], (LAYERS, D, HEADS * KEYS), D ** -0.5, 0.1875, ((0, 2), (1, 4), (2, 4))),
        "w_key": normal_values(streams_of[4], (LAYERS, D, HEADS * KEYS), D ** -0.5, 0.1875, ((0, 2), (1, 4), (2, 4))),
        "w_value": normal_values(streams_of[5], (LAYERS, D, HEADS * VALS), D ** -0.5, 0.1875, ((0, 2), (1, 4), (2, 4))),
        "w_gate": normal_values(streams_of[6], (LAYERS, D, HEADS * VALS), D ** -0.5, 0.1875, ((0, 2), (1, 4), (2, 4))),
        "w_decay": normal_values(streams_of[7], (LAYERS, D, 2 * HEADS), D ** -0.5, 0.1875, ((0, 2), (1, 4), (2, 4))),
        "conv_weight": normal_values(streams_of[8], (LAYERS, CONV, HEADS, 2 * KEYS + VALS), CONV ** -0.5, 3.0, ((0, 2),), jnp.float32),
        "head_rate": jnp.clip(-1.0 + 2.5 * jax.random.uniform(streams_of[9], (LAYERS, HEADS), jnp.float32) ** block_scale(streams_of[9], (LAYERS, HEADS), ((0, 2),), -0.2, 0.2), -1.0, 1.5),
        "head_bias": jnp.clip(-6.0 + 4.0 * jax.random.uniform(streams_of[10], (LAYERS, HEADS), jnp.float32) ** block_scale(streams_of[10], (LAYERS, HEADS), ((0, 2),), -0.2, 0.2), -6.0, -2.0),
        "out_gain": jnp.clip(1.0 + 0.1 * jax.random.normal(streams_of[11], (LAYERS, VALS), jnp.float32), 0.5, 1.5),
        "w_out": normal_values(streams_of[12], (LAYERS, HEADS * VALS, D), (HEADS * VALS // 4) ** -0.5, 0.25, ((0, 2), (1, 4), (2, 4))),
        "w_updown": normal_values(streams_of[13], (LAYERS, D, 2, FF), D ** -0.5, 0.1875, ((0, 2), (1, 4), (3, 4))),
        "w_down": normal_values(streams_of[14], (LAYERS, FF, D), FF ** -0.5, 0.109375, ((0, 2), (1, 4), (2, 4))),
        "cotangent": normal_values(streams_of[15], (MICRO, TOKENS, D), 1.0, 6.0, ((1, 16),)),
    }


@jax.custom_vjp
def low(v):
    return lax.optimization_barrier(v.astype(jnp.bfloat16)).astype(jnp.float32)

@jax.custom_vjp
def low_back(v):
    return v

def low_keep(v):
    return (low(v), None)

def low_pass(kept, grad):
    return (grad,)

def back_keep(v):
    return (v, None)

def back_low(kept, grad):
    return (low(grad),)
low.defvjp(low_keep, low_pass)
low_back.defvjp(back_keep, back_low)

def matmul(left, right):
    return jnp.dot(left.astype(jnp.float32), right.astype(jnp.float32), precision=lax.Precision.HIGHEST, preferred_element_type=jnp.float32)

def rms_norm(hidden, gain):
    return hidden * lax.rsqrt(lax.optimization_barrier(jnp.mean(hidden * hidden, axis=-1, keepdims=True)) + 1e-06) * gain

def layout(lengths_row, buffer):
    ends = jnp.cumsum(lengths_row.astype(jnp.int32), dtype=jnp.int32)
    token = jnp.arange(buffer, dtype=jnp.int32)
    start = lax.optimization_barrier(jnp.max(jnp.where(ends[None, :] <= token[:, None], ends[None, :], jnp.int32(0)), axis=1)).astype(jnp.int32)
    position = (token - start).astype(jnp.int32)
    live = (token < ends[-1]).astype(jnp.float32)
    reset = (position[::BLOCK] == 0).astype(jnp.float32)
    return (live, position, reset)

def mixer_core(proj_query, proj_key, proj_value, proj_gate, proj_decay, conv_part, rate_part, bias_part, gain_part, position, reset):
    maximum_precision = lax.Precision.HIGHEST
    rows = proj_query.shape[0]
    heads_here = conv_part.shape[1]
    key_size = proj_query.shape[1] // heads_here
    value_size = proj_value.shape[1] // heads_here
    stacked = jnp.concatenate([proj_query.reshape(rows, heads_here, key_size), proj_key.reshape(rows, heads_here, key_size), proj_value.reshape(rows, heads_here, value_size)], axis=2)
    convolved = jnp.zeros(stacked.shape, stacked.dtype)
    for lag in range(conv_part.shape[0]):
        moved = jnp.pad(stacked, ((lag, 0), (0, 0), (0, 0)))[:rows]
        keep = (position >= lag).astype(stacked.dtype)[:, None, None]
        convolved = convolved + conv_part[lag][None] * moved * keep
    convolved = jax.nn.silu(convolved)
    query = convolved[..., :key_size]
    keys = convolved[..., key_size:2 * key_size]
    values = convolved[..., 2 * key_size:]
    query = query * lax.rsqrt(lax.optimization_barrier(jnp.sum(query * query, axis=-1, keepdims=True)) + 1e-06) * key_size ** (-0.5)
    keys = keys * lax.rsqrt(lax.optimization_barrier(jnp.sum(keys * keys, axis=-1, keepdims=True)) + 1e-06)
    decay_in = proj_decay.reshape(rows, heads_here, 2)
    log_decay = -jnp.exp(rate_part) * jax.nn.softplus(decay_in[..., 0] + bias_part)
    strength = jax.nn.sigmoid(decay_in[..., 1])
    blocks = rows // BLOCK

    def to_blocks(array):
        return array.reshape(blocks, BLOCK, heads_here, -1).transpose(0, 2, 1, 3)
    query_blocks = to_blocks(query)
    key_blocks = to_blocks(keys)
    value_blocks = to_blocks(values)
    log_blocks = log_decay.reshape(blocks, BLOCK, heads_here).transpose(0, 2, 1)
    strength_blocks = strength.reshape(blocks, BLOCK, heads_here).transpose(0, 2, 1)
    cumlog = jnp.cumsum(log_blocks, axis=-1)
    lower = jnp.tril(jnp.ones((BLOCK, BLOCK), jnp.float32)) > 0.5
    strict = jnp.tril(jnp.ones((BLOCK, BLOCK), jnp.float32), -1) > 0.5
    spread = cumlog[..., :, None] - cumlog[..., None, :]
    ratio = jnp.where(lower, jnp.exp(jnp.where(lower, spread, 0.0)), 0.0)
    inner = jnp.einsum('nhik,nhjk->nhij', key_blocks, key_blocks, precision=maximum_precision)
    system = jnp.eye(BLOCK, dtype=inner.dtype) + jnp.where(strict, strength_blocks[..., :, None] * inner * ratio, 0.0)
    scaled_keys = key_blocks * (jnp.exp(cumlog) * strength_blocks)[..., None]
    scaled_values = value_blocks * strength_blocks[..., None]
    solved = lax.linalg.triangular_solve(system, jnp.concatenate([scaled_keys, scaled_values], axis=-1), left_side=True, lower=True, unit_diagonal=True)
    weight_part = solved[..., :key_size]
    update_part = solved[..., key_size:]
    scores = jnp.einsum('nhik,nhjk->nhij', query_blocks, key_blocks, precision=maximum_precision) * ratio
    query_decayed = query_blocks * jnp.exp(cumlog)[..., None]
    key_tail = key_blocks * jnp.exp(cumlog[..., -1:] - cumlog)[..., None]
    last = jnp.exp(cumlog[..., -1])

    def advance(running_state, pieces):
        weight_block_tile, update_block_tile, query_block_tile, score_block_tile, trailing_block, final_block, reset_blk = pieces
        running_state = running_state * (1.0 - reset_blk)
        new_state_value = update_block_tile - jnp.einsum('sny,syj->snj', weight_block_tile, running_state, precision=maximum_precision)
        block_outcome = jnp.einsum('sny,syj->snj', query_block_tile, running_state, precision=maximum_precision) + jnp.einsum('okp,opx->okx', score_block_tile, new_state_value, precision=maximum_precision)
        running_state = final_block[:, None, None] * running_state + jnp.einsum('nbt,nbu->ntu', trailing_block, new_state_value, precision=maximum_precision)
        return (running_state, block_outcome)
    initial = jnp.zeros((heads_here, key_size, value_size), update_part.dtype)
    unused, results = lax.scan(jax.checkpoint(advance), initial, (weight_part, update_part, query_decayed, scores, key_tail, last, reset.astype(update_part.dtype)))
    heads_out = results.transpose(0, 2, 1, 3).reshape(rows, heads_here, value_size)
    normed = heads_out * lax.rsqrt(lax.optimization_barrier(jnp.mean(heads_out * heads_out, axis=-1, keepdims=True)) + 1e-06) * gain_part
    gating = jax.nn.silu(proj_gate.reshape(rows, heads_here, value_size))
    return (normed * gating).reshape(rows, heads_here * value_size)

def layer_forward(weights, hidden, live, position, reset):
    norm_gain, w_query, w_key, w_value, w_gate, w_decay, conv_weight, head_rate, head_bias, out_gain, w_out, w_updown, w_down = weights
    normed = low(rms_norm(hidden, norm_gain[0]))
    proj_query = low_back(matmul(normed, w_query))
    proj_key = low_back(matmul(normed, w_key))
    proj_value = low_back(matmul(normed, w_value))
    proj_gate = low_back(matmul(normed, w_gate))
    proj_decay = low_back(matmul(normed, w_decay))
    mixed = low(mixer_core(proj_query, proj_key, proj_value, proj_gate, proj_decay, conv_weight, head_rate, head_bias, out_gain, position, reset))
    branch = low_back(matmul(mixed, w_out))
    after = hidden + live[:, None] * branch
    normed_two = low(rms_norm(after, norm_gain[1]))
    updown = low_back(jnp.einsum('td,dgf->tgf', normed_two, w_updown, precision=lax.Precision.HIGHEST))
    active = low(jax.nn.silu(updown[:, 0]) * updown[:, 1])
    ffn = low_back(matmul(active, w_down))
    return after + live[:, None] * ffn

def reference(inputs, lengths, norm_gain, w_query, w_key, w_value, w_gate, w_decay, conv_weight, head_rate, head_bias, out_gain, w_out, w_updown, w_down, cotangent):
    params = tuple((array.astype(jnp.float32) for array in (norm_gain, w_query, w_key, w_value, w_gate, w_decay, conv_weight, head_rate, head_bias, out_gain, w_out, w_updown, w_down)))
    hidden_all = inputs.astype(jnp.float32).reshape(MICRO * N_DP, BUF, D)
    buffer_lengths = lengths.astype(jnp.int32).reshape(MICRO * N_DP, SLOTS)

    def forward(weights, hidden_all):

        def one_buffer(pair):
            hidden, lengths_row = pair
            live, position, reset = layout(lengths_row, BUF)
            live = live.astype(hidden.dtype)
            for layer in range(LAYERS):
                hidden = low_back(hidden)
                hidden = low(layer_forward(tuple((weight[layer] for weight in weights)), hidden, live, position, reset))
            return hidden
        return lax.map(jax.checkpoint(one_buffer), (hidden_all, buffer_lengths))
    block_outcome, pullback = jax.vjp(forward, params, hidden_all)
    param_grads, hidden_grad = pullback(cotangent.astype(jnp.float32).reshape(MICRO * N_DP, BUF, D))
    whole = (MICRO, TOKENS, D)
    return (block_outcome.reshape(whole).astype(jnp.bfloat16), hidden_grad.reshape(whole).astype(jnp.bfloat16), param_grads[0], param_grads[1], param_grads[2], param_grads[3], param_grads[4], param_grads[5], param_grads[6], param_grads[7], param_grads[8], param_grads[9], param_grads[10], param_grads[11], param_grads[12])
```

```python
import jax
import jax.numpy as jnp
from jax import lax
from jax.experimental import pallas as pl
from jax.experimental.pallas import tpu as pltpu
from jax.sharding import PartitionSpec as P

KEYS = 128
BLOCK = 64
F32 = jnp.float32
LOW = jnp.bfloat16
VMEM_LIMIT = 56 * 1024 * 1024


def _dot(left, right, dims):
    return lax.dot_general(
        left.astype(LOW), right.astype(LOW), (dims, ((), ())), preferred_element_type=F32
    )


def mm(left, right):
    return _dot(left, right, ((1,), (0,)))


def mm_nt(left, right):
    return _dot(left, right, ((1,), (1,)))


def mm_tn(left, right):
    return _dot(left, right, ((0,), (0,)))


def exact(left, right, dims=((1,), (0,))):
    return lax.dot_general(
        left, right, (dims, ((), ())), precision=lax.Precision.HIGHEST, preferred_element_type=F32
    )


def mm_split(left, right):
    left_high = left.astype(LOW)
    right_high = right.astype(LOW)
    left_low = (left - left_high.astype(F32)).astype(LOW)
    right_low = (right - right_high.astype(F32)).astype(LOW)
    return mm(left_high, right_high) + (mm(left_high, right_low) + mm(left_low, right_high))


def grid_of(size):
    row = lax.broadcasted_iota(jnp.int32, (size, size), 0)
    col = lax.broadcasted_iota(jnp.int32, (size, size), 1)
    return row, col


def rowsum(array):
    return jnp.sum(array, axis=1, keepdims=True)


def unit_lower_inverse(below, row, col):
    ones = jnp.where(row == col, 1.0, 0.0)
    inverse = ones - jnp.where((row // 2 == col // 2), below, 0.0)
    half = 2
    while half < BLOCK:
        span = 2 * half
        part = (row // span == col // span) & (row % span >= half) & (col % span < half)
        piece = jnp.where(part, below, 0.0)
        inverse = inverse - mm_split(inverse, mm_split(piece, inverse))
        half = span
    return inverse


def convolve(own, before, taps):
    padded = jnp.concatenate([before, own], axis=0)
    shifted = [own]
    total = taps[0:1] * own
    for lag in range(1, taps.shape[0]):
        moved = pltpu.roll(padded, lag, 0)[8:]
        shifted.append(moved)
        total = total + taps[lag : lag + 1] * moved
    return shifted, total


def decay_of(pair, rate_exp, bias, row, col):
    shifted = pair[:, 0:1] + bias
    soft = jnp.maximum(shifted, 0.0) + jnp.log1p(jnp.exp(-jnp.abs(shifted)))
    log_decay = -rate_exp * soft
    strength = jax.nn.sigmoid(pair[:, 1:2])
    lower = jnp.where(row >= col, 1.0, 0.0)
    after = jnp.where(row > col, 1.0, 0.0)
    spread = exact(lower, log_decay * after)
    cumlog = spread[:, 0:1] + log_decay[0:1]
    ratio = jnp.where(row >= col, jnp.exp(spread), 0.0)
    return shifted, log_decay, strength, cumlog, ratio


def unit(array, scale=1.0):
    inv = lax.rsqrt(rowsum(array * array) + 1e-06)
    return array * inv, inv * scale


def mixer_forward_kernel(meta, params, mine, other, taps, gain, mixed_a, mixed_b, o_a, o_b, states, inverses, state, carry):
    step = pl.program_id(0)
    groups = mine.shape[0] // BLOCK
    row, col = grid_of(BLOCK)

    @pl.when(step == 0)
    def _():
        state[...] = jnp.zeros_like(state)
        carry[...] = jnp.zeros_like(carry)

    sources = (mine, other)
    outs = (mixed_a, mixed_b)
    os = (o_a, o_b)
    prepared = {}
    for head in range(2):
        source = sources[head]
        for block in range(groups):
            rows = pl.ds(block * BLOCK, BLOCK)
            keep = 1.0 - meta[1 + step * groups + block].astype(F32)
            own = source[rows, 0 : 4 * KEYS]
            if block == 0:
                before = carry[head]
            else:
                before = source[pl.ds(block * BLOCK - 8, 8), 0 : 4 * KEYS]
            _, conv = convolve(own, before * keep, taps[head])
            active = conv * jax.nn.sigmoid(conv)
            query, _ = unit(active[:, :KEYS])
            query = query * KEYS ** (-0.5)
            keys, _ = unit(active[:, KEYS : 2 * KEYS])
            values = active[:, 2 * KEYS :]
            _, _, strength, cumlog, ratio = decay_of(
                source[rows, 6 * KEYS : 6 * KEYS + 2], params[head, 0], params[head, 1], row, col
            )
            gamma = jnp.exp(cumlog)
            last = cumlog[BLOCK - 1 :]
            both = mm_nt(jnp.concatenate([keys, query], axis=0), keys)
            below = jnp.where(row > col, strength * ratio * both[:BLOCK], 0.0)
            inverse = unit_lower_inverse(below, row, col)
            inverses[block, head] = inverse
            weight = mm(inverse, (strength * gamma) * keys).astype(LOW)
            update = mm(inverse, strength * values)
            scores = (both[BLOCK:] * ratio).astype(LOW)
            tail = (keys * jnp.exp(last - cumlog)).astype(LOW)
            prepared[block, head] = (
                weight,
                update,
                scores,
                tail,
                (query * gamma).astype(LOW),
                jnp.exp(last),
                keep,
            )
        carry[head] = source[pl.ds(groups * BLOCK - 8, 8), 0 : 4 * KEYS]
    current = [state[0], state[1]]
    for block in range(groups):
        for head in range(2):
            weight, update, scores, tail, query_low, last, keep = prepared[block, head]
            held = current[head] * keep
            held_low = held.astype(LOW)
            states[block, head] = held_low
            fresh = (update - mm(weight, held_low)).astype(LOW)
            current[head] = last * held + mm_tn(tail, fresh)
            rows = pl.ds(block * BLOCK, BLOCK)
            outcome = mm(query_low, held_low) + mm(scores, fresh)
            os[head][rows, :] = outcome
            inv = lax.rsqrt(jnp.mean(outcome * outcome, axis=1, keepdims=True) + 1e-06)
            gate = sources[head][rows, 4 * KEYS : 6 * KEYS]
            mixed = outcome * inv * gain[...] * (gate * jax.nn.sigmoid(gate))
            outs[head][rows, :] = mixed.astype(LOW)
    state[0] = current[0]
    state[1] = current[1]


def mixer_backward_kernel(
    meta, params, mine, other, edge_a, edge_b, o_a, o_b, dm_a, dm_b, states, inverses, taps, gain,
    d_mine, d_other, d_taps, d_gain, d_params, state_grad, carry,
):
    step = pl.program_id(0)
    seq = pl.num_programs(0) - 1 - step
    groups = mine.shape[0] // BLOCK
    row, col = grid_of(BLOCK)

    @pl.when(step == 0)
    def _():
        state_grad[...] = jnp.zeros_like(state_grad)
        carry[...] = jnp.zeros_like(carry)
        d_taps[...] = jnp.zeros_like(d_taps)
        d_gain[...] = jnp.zeros_like(d_gain)
        d_params[...] = jnp.zeros_like(d_params)

    sources = (mine, other)
    edges = (edge_a, edge_b)
    os = (o_a, o_b)
    dms = (dm_a, dm_b)
    dsts = (d_mine, d_other)
    lower = jnp.where(row >= col, 1.0, 0.0)
    after = jnp.where(row > col, 1.0, 0.0)
    kept = {}
    gain_total = jnp.zeros((1, 2 * KEYS), F32)
    for head in range(2):
        source = sources[head]
        for block in range(groups):
            rows = pl.ds(block * BLOCK, BLOCK)
            keep = 1.0 - meta[1 + seq * groups + block].astype(F32)
            own = source[rows, 0 : 4 * KEYS]
            if block == 0:
                before = edges[head][:, 0 : 4 * KEYS]
            else:
                before = source[pl.ds(block * BLOCK - 8, 8), 0 : 4 * KEYS]
            shifted, conv = convolve(own, before * keep, taps[head])
            sig = jax.nn.sigmoid(conv)
            active = conv * sig
            slope = sig * (1.0 + conv * (1.0 - sig))
            query_unit, query_inv = unit(active[:, :KEYS])
            query = query_unit * KEYS ** (-0.5)
            keys, keys_inv = unit(active[:, KEYS : 2 * KEYS])
            values = active[:, 2 * KEYS :]
            decay_pre, log_decay, strength, cumlog, ratio = decay_of(
                source[rows, 6 * KEYS : 6 * KEYS + 2], params[head, 0], params[head, 1], row, col
            )
            gamma = jnp.exp(cumlog)
            last = cumlog[BLOCK - 1 :]
            tail_scale = jnp.exp(last - cumlog)
            both = mm_nt(jnp.concatenate([keys, query], axis=0), keys)
            near = jnp.where(row > col, ratio * both[:BLOCK], 0.0)
            scores = both[BLOCK:] * ratio
            inverse = inverses[block, head].astype(LOW)
            held = states[block, head]
            weight = mm(inverse, (strength * gamma) * keys).astype(LOW)
            key_state = mm(keys, held)
            lacking = values - gamma * key_state
            fresh = mm(inverse, strength * lacking)
            outcome = os[head][rows, :]
            d_mixed = dms[head][rows, :]
            gate = source[rows, 4 * KEYS : 6 * KEYS]
            gate_sig = jax.nn.sigmoid(gate)
            gate_act = gate * gate_sig
            inv = lax.rsqrt(jnp.mean(outcome * outcome, axis=1, keepdims=True) + 1e-06)
            normed = outcome * inv
            weighted = d_mixed * gain[...]
            d_gate = weighted * normed * (gate_sig * (1.0 + gate * (1.0 - gate_sig)))
            dsts[head][rows, 4 * KEYS : 6 * KEYS] = d_gate.astype(LOW)
            gain_total = gain_total + jnp.sum(d_mixed * normed * gate_act, axis=0, keepdims=True)
            d_normed = weighted * gate_act
            d_out = inv * (d_normed - normed * jnp.mean(d_normed * normed, axis=1, keepdims=True))
            d_out_low = d_out.astype(LOW)
            part_fresh = mm_tn(scores, d_out_low)
            part_state = mm_tn(query * gamma, d_out_low)
            tail = keys * tail_scale
            kept[block, head] = dict(
                keep=keep, shifted=shifted, slope=slope, query_unit=query_unit, query_inv=query_inv,
                query=query, keys=keys, keys_inv=keys_inv, decay_pre=decay_pre, log_decay=log_decay,
                strength=strength, ratio=ratio, gamma=gamma, last=jnp.exp(last), tail=tail,
                tail_scale=tail_scale, near=near, scores=scores, inverse=inverse, held=held,
                weight=weight, key_state=key_state, lacking=lacking, fresh=fresh,
                d_out_low=d_out_low, part_fresh=part_fresh, part_state=part_state,
            )
    d_gain[...] += gain_total
    current = [state_grad[0], state_grad[1]]
    for block in reversed(range(groups)):
        for head in range(2):
            k = kept[block, head]
            k["ds"] = current[head]
            d_fresh = (k["part_fresh"] + mm(k["tail"], current[head])).astype(LOW)
            k["d_fresh"] = d_fresh
            below = k["last"] * current[head] + k["part_state"] - mm_tn(k["weight"], d_fresh)
            current[head] = below * k["keep"]
    state_grad[0] = current[0]
    state_grad[1] = current[1]
    for head in range(2):
        next_rows = carry[head]
        taps_here = taps[head]
        tap_sums = [jnp.zeros((1, 4 * KEYS), F32) for _ in range(4)]
        rate_sum = jnp.zeros((1, 1), F32)
        bias_sum = jnp.zeros((1, 1), F32)
        for block in reversed(range(groups)):
            rows = pl.ds(block * BLOCK, BLOCK)
            k = kept[block, head]
            keys, query, gamma, strength = k["keys"], k["query"], k["gamma"], k["strength"]
            fresh_low = k["fresh"].astype(LOW)
            ds_low = k["ds"].astype(LOW)
            d_fill = mm_tn(k["inverse"], k["d_fresh"])
            grams = mm_nt(jnp.concatenate([d_fill.astype(LOW), k["d_out_low"]], axis=0), fresh_low)
            d_below = jnp.where(row > col, -grams[:BLOCK], 0.0)
            d_scores = grams[BLOCK:]
            d_tail = mm_nt(fresh_low, ds_low)
            scaled = (strength * gamma) * d_fill
            through = mm_nt(jnp.concatenate([k["d_out_low"], scaled.astype(LOW)], axis=0), k["held"])
            d_qk = (d_scores * k["ratio"]).astype(LOW)
            d_kk = (strength * d_below * k["ratio"]).astype(LOW)
            pair = mm(jnp.concatenate([d_qk, d_kk], axis=0), keys)
            d_query = gamma * through[:BLOCK] + pair[:BLOCK]
            d_keys = (
                pair[BLOCK:]
                - through[BLOCK:]
                + k["tail_scale"] * d_tail
                + mm_tn(jnp.concatenate([d_qk, d_kk], axis=0), jnp.concatenate([query, keys], axis=0))
            )
            d_values = strength * d_fill
            d_strength = rowsum(d_fill * k["lacking"]) + rowsum(d_below * k["near"])
            spread_grad = d_scores * k["scores"] + strength * d_below * k["near"]
            tail_part = rowsum(d_tail * k["tail"])
            d_cum = gamma * rowsum(query * through[:BLOCK]) - rowsum(scaled * k["key_state"]) - tail_part
            at_last = jnp.sum(tail_part, axis=0, keepdims=True) + k["last"] * jnp.sum(
                rowsum(k["ds"] * k["held"].astype(F32)), axis=0, keepdims=True
            )
            place = lax.broadcasted_iota(jnp.int32, (BLOCK, 1), 0)
            d_cum = d_cum + jnp.where(place == BLOCK - 1, at_last, 0.0)
            spread_grad = spread_grad + jnp.where(col == 0, d_cum, 0.0)
            d_log = rowsum(exact(lower, spread_grad, ((0,), (0,))) * after)
            d_log = d_log + jnp.where(place == 0, jnp.sum(d_cum, axis=0, keepdims=True), 0.0)
            d_decay = d_log * (-params[head, 0]) * jax.nn.sigmoid(k["decay_pre"])
            rate_sum = rate_sum + jnp.sum(d_log * k["log_decay"], axis=0, keepdims=True)
            bias_sum = bias_sum + jnp.sum(d_decay, axis=0, keepdims=True)
            d_write = d_strength * strength * (1.0 - strength)
            dsts[head][rows, 6 * KEYS : 6 * KEYS + 2] = jnp.concatenate([d_decay, d_write], axis=1).astype(LOW)
            d_query = d_query * KEYS ** (-0.5)
            unit_q = k["query_unit"]
            d_active = jnp.concatenate(
                [
                    k["query_inv"] * (d_query - unit_q * rowsum(unit_q * d_query)),
                    k["keys_inv"] * (d_keys - keys * rowsum(keys * d_keys)),
                    d_values,
                ],
                axis=1,
            )
            d_conv = d_active * k["slope"]
            padded = jnp.concatenate([d_conv, next_rows], axis=0)
            d_own = taps_here[0:1] * d_conv
            tap_sums[0] = tap_sums[0] + jnp.sum(d_conv * k["shifted"][0], axis=0, keepdims=True)
            for lag in range(1, 4):
                moved = pltpu.roll(padded, BLOCK + 8 - lag, 0)[:BLOCK]
                d_own = d_own + taps_here[lag : lag + 1] * moved
                tap_sums[lag] = tap_sums[lag] + jnp.sum(
                    d_conv * k["shifted"][lag], axis=0, keepdims=True
                )
            dsts[head][rows, 0 : 4 * KEYS] = d_own.astype(LOW)
            next_rows = d_conv[0:8] * k["keep"]
        carry[head] = next_rows
        for lag in range(4):
            d_taps[head, lag : lag + 1, :] += tap_sums[lag]
        lane = lax.broadcasted_iota(jnp.int32, (1, KEYS), 1)
        d_params[head : head + 1, :] += jnp.where(lane == 0, rate_sum, 0.0) + jnp.where(
            lane == 1, bias_sum, 0.0
        )


def mixer_forward(meta, params, mine, other, taps, gain, parts):
    rows = mine.shape[0]
    wide = mine.shape[1]
    group = rows // parts
    per = group // BLOCK

    def place(step, meta):
        return (step ^ meta[0], 0)

    def stacked(step, meta):
        return (step, 0, 0, 0)

    vals = 2 * KEYS
    row_spec = pl.BlockSpec((group, vals), place)
    return pl.pallas_call(
        mixer_forward_kernel,
        grid_spec=pltpu.PrefetchScalarGridSpec(
            num_scalar_prefetch=1,
            grid=(parts,),
            in_specs=[
                pl.BlockSpec(memory_space=pltpu.SMEM),
                pl.BlockSpec((group, wide), place),
                pl.BlockSpec((group, wide), place),
                pl.BlockSpec((2, 4, 4 * KEYS), lambda step, meta: (0, 0, 0)),
                pl.BlockSpec((1, vals), lambda step, meta: (0, 0)),
            ],
            out_specs=[
                row_spec,
                row_spec,
                row_spec,
                row_spec,
                pl.BlockSpec((per, 2, KEYS, vals), stacked),
                pl.BlockSpec((per, 2, BLOCK, BLOCK), stacked),
            ],
            scratch_shapes=[pltpu.VMEM((2, KEYS, vals), F32), pltpu.VMEM((2, 8, 4 * KEYS), F32)],
        ),
        out_shape=[
            jax.ShapeDtypeStruct((rows, vals), LOW),
            jax.ShapeDtypeStruct((rows, vals), LOW),
            jax.ShapeDtypeStruct((rows, vals), F32),
            jax.ShapeDtypeStruct((rows, vals), F32),
            jax.ShapeDtypeStruct((rows // BLOCK, 2, KEYS, vals), LOW),
            jax.ShapeDtypeStruct((rows // BLOCK, 2, BLOCK, BLOCK), F32),
        ],
        compiler_params=pltpu.CompilerParams(vmem_limit_bytes=VMEM_LIMIT),
        name="mixer_forward",
    )(meta, params, mine, other, taps, gain)


def mixer_backward(meta, params, mine, other, o_a, o_b, dm_a, dm_b, states, inverses, taps, gain, parts):
    rows = mine.shape[0]
    wide = mine.shape[1]
    group = rows // parts
    per = group // BLOCK

    def place(step, meta):
        return ((parts - 1 - step) ^ meta[0], 0)

    def edge(step, meta):
        return ((jnp.maximum(parts - 2 - step, 0) ^ meta[0]) * (group // 8) + group // 8 - 1, 0)

    def stacked(step, meta):
        return (parts - 1 - step, 0, 0, 0)

    vals = 2 * KEYS
    row_spec = pl.BlockSpec((group, vals), place)
    wide_spec = pl.BlockSpec((group, wide), place)
    edge_spec = pl.BlockSpec((8, wide), edge)
    taps_spec = pl.BlockSpec((2, 4, 4 * KEYS), lambda step, meta: (0, 0, 0))
    gain_spec = pl.BlockSpec((1, vals), lambda step, meta: (0, 0))
    return pl.pallas_call(
        mixer_backward_kernel,
        grid_spec=pltpu.PrefetchScalarGridSpec(
            num_scalar_prefetch=1,
            grid=(parts,),
            in_specs=[
                pl.BlockSpec(memory_space=pltpu.SMEM),
                wide_spec,
                wide_spec,
                edge_spec,
                edge_spec,
                row_spec,
                row_spec,
                row_spec,
                row_spec,
                pl.BlockSpec((per, 2, KEYS, vals), stacked),
                pl.BlockSpec((per, 2, BLOCK, BLOCK), stacked),
                taps_spec,
                gain_spec,
            ],
            out_specs=[
                wide_spec,
                wide_spec,
                taps_spec,
                gain_spec,
                pl.BlockSpec((2, KEYS), lambda step, meta: (0, 0)),
            ],
            scratch_shapes=[pltpu.VMEM((2, KEYS, vals), F32), pltpu.VMEM((2, 8, 4 * KEYS), F32)],
        ),
        out_shape=[
            jax.ShapeDtypeStruct((rows, wide), LOW),
            jax.ShapeDtypeStruct((rows, wide), LOW),
            jax.ShapeDtypeStruct((2, 4, 4 * KEYS), F32),
            jax.ShapeDtypeStruct((1, vals), F32),
            jax.ShapeDtypeStruct((2, KEYS), F32),
        ],
        compiler_params=pltpu.CompilerParams(vmem_limit_bytes=VMEM_LIMIT),
        name="mixer_backward",
    )(meta, params, mine, other, mine, other, o_a, o_b, dm_a, dm_b, states, inverses, taps, gain)


def swap_section(array):
    return lax.ppermute(array, "section", [(0, 1), (1, 0)])


def send_by(array, offset):
    peers = lax.axis_size("tensor")
    return lax.ppermute(array, "tensor", [(i, i ^ offset) for i in range(peers)])


def spread_rows(values):
    peers = lax.axis_size("tensor")
    return [values] + [send_by(values, k) for k in range(1, peers)]


def collect_rows(parts):
    total = parts[0]
    for k in range(1, len(parts)):
        total = total + send_by(parts[k].astype(LOW), k).astype(F32)
    return total


def nn(left, right):
    return jnp.dot(left, right, preferred_element_type=F32)


def nt(left, right):
    return lax.dot_general(left, right, (((1,), (1,)), ((), ())), preferred_element_type=F32)


def tn(left, right):
    return lax.dot_general(left, right, (((0,), (0,)), ((), ())), preferred_element_type=F32)


def norm_forward(hidden, gain):
    inv = lax.rsqrt(jnp.mean(hidden * hidden, axis=-1, keepdims=True) + 1e-06)
    return (hidden * inv * gain).astype(LOW), inv


def norm_backward(hidden, inv, gain, grad):
    normed = hidden * inv
    weighted = grad * gain
    back = inv * (weighted - normed * jnp.mean(weighted * normed, axis=-1, keepdims=True))
    return back, jnp.sum(grad * normed, axis=0)


def layout(lengths_row, buffer):
    ends = jnp.cumsum(lengths_row, dtype=jnp.int32)
    token = jnp.arange(buffer, dtype=jnp.int32)
    start = jnp.max(jnp.where(ends[None, :] <= token[:, None], ends[None, :], 0), axis=1)
    live = (token < ends[-1]).astype(F32)
    reset = ((token - start)[::BLOCK] == 0).astype(jnp.int32)
    return live, reset


def split_rows(array, count):
    size = array.shape[0] // count
    return [array[k * size : (k + 1) * size] for k in range(count)]


def layer_forward(hidden, weights, gains, small, meta, live):
    mix_mine, mix_other, out_mine, out_other, up_mine, up_other, down_mine, down_other = weights
    params, taps, gain_out = small
    peers = lax.axis_size("tensor")
    normed, inv_one = norm_forward(hidden, gains[0])
    normed_all = jnp.concatenate(spread_rows(normed), axis=0)
    mine = nn(normed_all, mix_mine)
    other = nn(normed_all, mix_other)
    mixed_a, mixed_b, o_a, o_b, states, inverses = mixer_forward(
        meta, params, mine, other, taps, gain_out, peers
    )
    branch = collect_rows(
        [
            nt(a, out_mine) + nt(b, out_other)
            for a, b in zip(split_rows(mixed_a, peers), split_rows(mixed_b, peers))
        ]
    )
    after = hidden + live * branch
    normed_two, inv_two = norm_forward(after, gains[1])
    normed_two_all = spread_rows(normed_two)
    half = down_mine.shape[1]
    ups, actives, ffn = [], [], []
    for chunk in normed_two_all:
        pair = (nn(chunk, up_mine), nn(chunk, up_other))
        active = [(jax.nn.silu(u[:, :half]) * u[:, half:]).astype(LOW) for u in pair]
        ups.append(pair)
        actives.append(active)
        ffn.append(nt(active[0], down_mine) + nt(active[1], down_other))
    result = after + live * collect_rows(ffn)
    kept = (
        hidden, inv_one, normed_all, mine, other, o_a, o_b, states, inverses, mixed_a, mixed_b,
        after, inv_two, normed_two_all, ups, actives,
    )
    return result, kept


def layer_backward(grad, kept, weights, gains, small, meta, live, owners):
    mix_mine, mix_other, out_mine, out_other, up_mine, up_other, down_mine, down_other = weights
    params, taps, gain_out = small
    (
        hidden, inv_one, normed_all, mine, other, o_a, o_b, states, inverses, mixed_a, mixed_b,
        after, inv_two, normed_two_all, ups, actives,
    ) = kept
    peers = lax.axis_size("tensor")
    half = down_mine.shape[1]
    ffn_grads = spread_rows((live * grad).astype(LOW))
    d_ups, back = ([], []), []
    for chunk, pair in zip(ffn_grads, ups):
        partial = None
        for side, (u, down, up) in enumerate(
            ((pair[0], down_mine, up_mine), (pair[1], down_other, up_other))
        ):
            d_active = nn(chunk, down)
            gate, lift = u[:, :half], u[:, half:]
            sig = jax.nn.sigmoid(gate)
            d_gate = d_active * lift * (sig * (1.0 + gate * (1.0 - sig)))
            d_lift = d_active * (gate * sig)
            d_up = jnp.concatenate([d_gate, d_lift], axis=1).astype(LOW)
            d_ups[side].append(d_up)
            piece = nt(d_up, up)
            partial = piece if partial is None else partial + piece
        back.append(partial)
    back_two = collect_rows(back)
    two_all = jnp.concatenate(normed_two_all, axis=0)
    ffn_all = jnp.concatenate(ffn_grads, axis=0)
    ffn_parts = []
    for side in range(2):
        d_up_all = jnp.concatenate(d_ups[side], axis=0)
        active_all = jnp.concatenate([pair[side] for pair in actives], axis=0)
        ffn_parts.append((tn(two_all, d_up_all), tn(ffn_all, active_all)))
    ffn_owned = owners(*[jnp.concatenate(part, axis=1) for part in ffn_parts])
    back, gain_two_grad = norm_backward(after, inv_two, gains[1], back_two)
    grad_after = grad + back
    branch_all = jnp.concatenate(spread_rows((live * grad_after).astype(LOW)), axis=0)
    d_mine, d_other, d_taps, d_gain, d_params = mixer_backward(
        meta, params, mine, other, o_a, o_b, nn(branch_all, out_mine), nn(branch_all, out_other),
        states, inverses, taps, gain_out, peers,
    )
    back_one = collect_rows(
        [
            nt(a, mix_mine) + nt(b, mix_other)
            for a, b in zip(split_rows(d_mine, peers), split_rows(d_other, peers))
        ]
    )
    out_parts = [tn(branch_all, mixed_a), tn(branch_all, mixed_b)]
    mix_parts = [tn(normed_all, d_mine), tn(normed_all, d_other)]
    mix_owned = owners(
        *[jnp.concatenate([o, m], axis=1) for o, m in zip(out_parts, mix_parts)]
    )
    back, gain_one_grad = norm_backward(hidden, inv_one, gains[0], back_one)
    return (
        grad_after + back,
        (ffn_owned, mix_owned),
        (jnp.stack([gain_one_grad, gain_two_grad]), d_taps, d_params, d_gain),
    )


def on_device(
    inputs, lengths, norm_gain, w_query, w_key, w_value, w_gate, w_decay, conv_weight, head_rate,
    head_bias, out_gain, w_out, w_updown, w_down, cotangent,
):
    section = lax.axis_index("section")
    layers = lax.axis_size("section")
    first = section == 0
    part = lax.axis_index("tensor")
    rows_here = inputs.shape[1]
    buffer = rows_here * lax.axis_size("tensor")
    ff = w_down.shape[1]
    half = ff // 2
    vals = 2 * KEYS

    def half_mix(h):
        return jnp.concatenate(
            [
                w_query[0][:, h * KEYS : (h + 1) * KEYS],
                w_key[0][:, h * KEYS : (h + 1) * KEYS],
                w_value[0][:, h * vals : (h + 1) * vals],
                w_gate[0][:, h * vals : (h + 1) * vals],
                w_decay[0][:, h * 2 : (h + 1) * 2],
            ],
            axis=1,
        )

    def half_rest(h):
        hidden_part = slice(h * half, (h + 1) * half)
        return jnp.concatenate(
            [
                w_updown[0][:, 0, hidden_part],
                w_updown[0][:, 1, hidden_part],
                w_down[0][hidden_part].T,
                w_out[0][h * vals : (h + 1) * vals].T,
            ],
            axis=1,
        )

    def both_layers(halves):
        keep = jnp.where(first, halves[0], halves[1])
        got = swap_section(jnp.where(first, halves[1], halves[0]))
        return jnp.where(first, keep, got), jnp.where(first, got, keep)

    mix_shards = both_layers((half_mix(0), half_mix(1)))
    rest_shards = both_layers((half_rest(0), half_rest(1)))

    def fetch(layer):
        sides = []
        mix = lax.all_gather(mix_shards[layer], "dp", axis=0, tiled=True)
        rest = lax.all_gather(rest_shards[layer], "dp", axis=0, tiled=True)
        return mix, swap_section(mix), rest, swap_section(rest)

    def arrange(fetched):
        mix, mix_two, rest, rest_two = fetched
        return (
            mix, mix_two,
            rest[:, 3 * half :], rest_two[:, 3 * half :],
            rest[:, : 2 * half], rest_two[:, : 2 * half],
            rest[:, 2 * half : 3 * half], rest_two[:, 2 * half : 3 * half],
        )

    def of_all(array):
        return lax.all_gather(array, "section", axis=0, tiled=True)

    gains_all = of_all(norm_gain)
    sizes = (conv_weight.size, head_rate.size, head_bias.size, out_gain.size)
    packed = of_all(
        jnp.concatenate(
            [conv_weight.reshape(-1), head_rate.reshape(-1), head_bias.reshape(-1), out_gain.reshape(-1)]
        )[None]
    )
    edges = [0]
    for size in sizes:
        edges.append(edges[-1] + size)
    heads = conv_weight.shape[2]
    places = [part * 2 + section, part * 2 + 1 - section]
    smalls = []
    for layer in range(2):
        conv, rate, bias, gain_out = (packed[layer, a:b] for a, b in zip(edges[:-1], edges[1:]))
        conv = conv.reshape(conv_weight.shape[1:])
        taps = jnp.concatenate(
            [lax.dynamic_slice_in_dim(conv, p, 1, 1) for p in places], axis=1
        ).transpose(1, 0, 2)
        scale = jnp.stack([jnp.exp(rate), bias], axis=1)
        params = jnp.concatenate([lax.dynamic_slice_in_dim(scale, p, 1, 0) for p in places], axis=0)
        smalls.append((params, taps, gain_out[None]))

    lengths_row = lax.dynamic_index_in_dim(lengths[:, 0], section, 0, keepdims=False)
    live_all, reset = layout(lengths_row, buffer)
    live = lax.dynamic_slice_in_dim(live_all, part * rows_here, rows_here)[:, None]
    meta = jnp.concatenate([part[None].astype(jnp.int32), reset])

    def own_micro(array):
        return lax.dynamic_index_in_dim(array, section, 0, keepdims=False).astype(F32)

    weights = [arrange(fetch(layer)) for layer in range(2)]
    hidden = own_micro(inputs)
    kept = []
    for layer in range(2):
        result, saved = layer_forward(hidden, weights[layer], gains_all[layer], smalls[layer], meta, live)
        result_low = result.astype(LOW)
        hidden = result_low.astype(F32)
        kept.append(saved)

    def owners(mine, other):
        got = swap_section(other.astype(LOW))
        total = (mine + got.astype(F32)).astype(LOW)
        return lax.psum_scatter(total, "dp", scatter_dimension=0, tiled=True)

    grad = own_micro(cotangent)
    owned, small_grads = [None, None], [None, None]
    for layer in (1, 0):
        grad, owned[layer], small_grads[layer] = layer_backward(
            grad, kept[layer], weights[layer], gains_all[layer], smalls[layer], meta, live, owners
        )
        grad_low = grad.astype(LOW)
        grad = grad_low.astype(F32)

    halves = []
    for kind in range(2):
        keep = jnp.where(first, owned[0][kind], owned[1][kind])
        got = swap_section(jnp.where(first, owned[1][kind], owned[0][kind]))
        halves.append(
            (
                jnp.where(first, keep, got).astype(F32),
                jnp.where(first, got, keep).astype(F32),
            )
        )
    ffn_pair, mix_pair = halves

    def columns(pair, start, size):
        return jnp.concatenate([side[:, start : start + size] for side in pair], axis=1)

    grad_updown = jnp.stack([columns(ffn_pair, 0, half), columns(ffn_pair, half, half)], axis=1)
    grad_down = columns(ffn_pair, 2 * half, half).T
    grad_out = columns(mix_pair, 0, vals).T
    grad_query = columns(mix_pair, vals, KEYS)
    grad_key = columns(mix_pair, vals + KEYS, KEYS)
    grad_value = columns(mix_pair, vals + 2 * KEYS, vals)
    grad_gate = columns(mix_pair, 2 * vals + 2 * KEYS, vals)
    grad_decay = columns(mix_pair, 3 * vals + 2 * KEYS, 2)

    flat = []
    for layer in range(2):
        gain_grads, d_taps, d_params, d_gain = small_grads[layer]
        conv_full = jnp.zeros(conv_weight.shape[1:], F32)
        pair_full = jnp.zeros((heads, 2), F32)
        for side, p in enumerate(places):
            conv_full = lax.dynamic_update_slice_in_dim(conv_full, d_taps[side][:, None, :], p, 1)
            pair_full = lax.dynamic_update_slice_in_dim(pair_full, d_params[side : side + 1, :2], p, 0)
        flat.append(
            jnp.concatenate(
                [
                    conv_full.reshape(-1), pair_full[:, 0], pair_full[:, 1], d_gain.reshape(-1),
                    gain_grads.reshape(-1),
                ]
            )
        )
    summed = lax.psum(jnp.stack(flat), ("section", "dp", "tensor"))
    own = lax.dynamic_index_in_dim(summed, section, 0, keepdims=False)
    pieces = [own[a:b] for a, b in zip(edges[:-1], edges[1:])]
    return (
        result_low[None],
        grad_low[None],
        own[edges[-1] :].reshape(norm_gain.shape),
        grad_query[None],
        grad_key[None],
        grad_value[None],
        grad_gate[None],
        grad_decay[None],
        pieces[0].reshape(conv_weight.shape),
        pieces[1].reshape(head_rate.shape),
        pieces[2].reshape(head_bias.shape),
        pieces[3].reshape(out_gain.shape),
        grad_out[None],
        grad_updown[None],
        grad_down[None],
    )


def solution(mesh):
    in_specs = (
        P(None, ("dp", "tensor"), None),
        P(None, "dp", None),
        P("section", None, None),
        P("section", "dp", "tensor"),
        P("section", "dp", "tensor"),
        P("section", "dp", "tensor"),
        P("section", "dp", "tensor"),
        P("section", "dp", "tensor"),
        P("section", None, None, None),
        P("section", None),
        P("section", None),
        P("section", None),
        P("section", "tensor", "dp"),
        P("section", "dp", None, "tensor"),
        P("section", "tensor", "dp"),
        P(None, ("dp", "tensor"), None),
    )
    out_specs = (
        P("section", ("dp", "tensor"), None),
        P("section", ("dp", "tensor"), None),
        P("section", None, None),
        P("section", "dp", "tensor"),
        P("section", "dp", "tensor"),
        P("section", "dp", "tensor"),
        P("section", "dp", "tensor"),
        P("section", "dp", "tensor"),
        P("section", None, None, None),
        P("section", None),
        P("section", None),
        P("section", None),
        P("section", "tensor", "dp"),
        P("section", "dp", None, "tensor"),
        P("section", "tensor", "dp"),
    )
    return jax.shard_map(
        on_device, mesh=mesh, in_specs=in_specs, out_specs=out_specs, check_vma=False
    )
```

```python
import jax
import jax.numpy as jnp
from jax import lax
from jax.experimental import pallas as pl
from jax.experimental.pallas import tpu as pltpu
from jax.sharding import PartitionSpec as P

KEYS = 128
BLOCK = 64
F32 = jnp.float32
LOW = jnp.bfloat16
VMEM_LIMIT = 56 * 1024 * 1024


def _dot(left, right, dims):
    return lax.dot_general(
        left.astype(LOW), right.astype(LOW), (dims, ((), ())), preferred_element_type=F32
    )


def mm(left, right):
    return _dot(left, right, ((1,), (0,)))


def mm_nt(left, right):
    return _dot(left, right, ((1,), (1,)))


def mm_tn(left, right):
    return _dot(left, right, ((0,), (0,)))


def exact(left, right, dims=((1,), (0,))):
    return lax.dot_general(
        left, right, (dims, ((), ())), precision=lax.Precision.HIGHEST, preferred_element_type=F32
    )


def mm_split(left, right):
    left_high = left.astype(LOW)
    right_high = right.astype(LOW)
    left_low = (left - left_high.astype(F32)).astype(LOW)
    right_low = (right - right_high.astype(F32)).astype(LOW)
    return mm(left_high, right_high) + (mm(left_high, right_low) + mm(left_low, right_high))


def grid_of(size):
    row = lax.broadcasted_iota(jnp.int32, (size, size), 0)
    col = lax.broadcasted_iota(jnp.int32, (size, size), 1)
    return row, col


def rowsum(array):
    return jnp.sum(array, axis=1, keepdims=True)


def unit_lower_inverses(belows, row, col):
    ones = jnp.where(row == col, 1.0, 0.0)
    near = row // 2 == col // 2
    inverses = [ones - jnp.where(near, below, 0.0) for below in belows]
    half = 2
    while half < BLOCK:
        span = 2 * half
        part = (row // span == col // span) & (row % span >= half) & (col % span < half)
        pieces = [mm_split(jnp.where(part, b, 0.0), i) for b, i in zip(belows, inverses)]
        inverses = [i - mm_split(i, p) for p, i in zip(pieces, inverses)]
        half = span
    return inverses


def convolve(own, before, taps):
    padded = jnp.concatenate([before, own], axis=0)
    shifted = [own]
    total = taps[0:1] * own
    for lag in range(1, taps.shape[0]):
        moved = pltpu.roll(padded, lag, 0)[8:]
        shifted.append(moved)
        total = total + taps[lag : lag + 1] * moved
    return shifted, total


def decay_of(pair, rate_exp, bias, row, col):
    shifted = pair[:, 0:1] + bias
    soft = jnp.maximum(shifted, 0.0) + jnp.log1p(jnp.exp(-jnp.abs(shifted)))
    log_decay = -rate_exp * soft
    strength = jax.nn.sigmoid(pair[:, 1:2])
    lower = jnp.where(row >= col, 1.0, 0.0)
    after = jnp.where(row > col, 1.0, 0.0)
    spread = exact(lower, log_decay * after)
    cumlog = spread[:, 0:1] + log_decay[0:1]
    ratio = jnp.where(row >= col, jnp.exp(spread), 0.0)
    return shifted, log_decay, strength, cumlog, ratio


def unit(array, scale=1.0):
    inv = lax.rsqrt(rowsum(array * array) + 1e-06)
    return array * inv, inv * scale


def mixer_forward_kernel(
    meta, params, normed, mix_mine, mix_other, taps, gain,
    mine, other, mixed_a, mixed_b, o_a, o_b, states, inverses, branch, state, carry,
):
    step = pl.program_id(0)
    groups = mine.shape[0] // BLOCK
    row, col = grid_of(BLOCK)

    @pl.when(step == 0)
    def _():
        state[...] = jnp.zeros_like(state)
        carry[...] = jnp.zeros_like(carry)

    mine[...] = mm(normed[...], mix_mine[:, : 7 * KEYS])
    other[...] = mm(normed[...], mix_other[:, : 7 * KEYS])
    sources = (mine, other)
    outs = (mixed_a, mixed_b)
    os = (o_a, o_b)
    prepared = {}
    for head in range(2):
        source = sources[head]
        for block in range(groups):
            rows = pl.ds(block * BLOCK, BLOCK)
            keep = 1.0 - meta[1 + step * groups + block].astype(F32)
            own = source[rows, 0 : 4 * KEYS]
            if block == 0:
                before = carry[head]
            else:
                before = source[pl.ds(block * BLOCK - 8, 8), 0 : 4 * KEYS]
            _, conv = convolve(own, before * keep, taps[head])
            active = conv * jax.nn.sigmoid(conv)
            query, _ = unit(active[:, :KEYS])
            query = query * KEYS ** (-0.5)
            keys, _ = unit(active[:, KEYS : 2 * KEYS])
            values = active[:, 2 * KEYS :]
            _, _, strength, cumlog, ratio = decay_of(
                source[rows, 6 * KEYS : 6 * KEYS + 2], params[head, 0], params[head, 1], row, col
            )
            gamma = jnp.exp(cumlog)
            last = cumlog[BLOCK - 1 :]
            both = mm_nt(jnp.concatenate([keys, query], axis=0), keys)
            below = jnp.where(row > col, strength * ratio * both[:BLOCK], 0.0)
            scores = (both[BLOCK:] * ratio).astype(LOW)
            tail = (keys * jnp.exp(last - cumlog)).astype(LOW)
            prepared[block, head] = (
                below,
                ((strength * gamma) * keys).astype(LOW),
                (strength * values).astype(LOW),
                scores,
                tail,
                (query * gamma).astype(LOW),
                jnp.exp(last),
                keep,
            )
        carry[head] = source[pl.ds(groups * BLOCK - 8, 8), 0 : 4 * KEYS]
    order = list(prepared)
    solved = unit_lower_inverses([prepared[place][0] for place in order], row, col)
    for place, inverse in zip(order, solved):
        inverse_low = inverse.astype(LOW)
        inverses[place[0], place[1]] = inverse_low
        _, scaled_keys, scaled_values, *rest = prepared[place]
        weight = mm(inverse_low, scaled_keys).astype(LOW)
        prepared[place] = (weight, mm(inverse_low, scaled_values), *rest)
    current = [state[0], state[1]]
    for block in range(groups):
        for head in range(2):
            weight, update, scores, tail, query_low, last, keep = prepared[block, head]
            held = current[head] * keep
            held_low = held.astype(LOW)
            states[block, head] = held_low
            fresh = (update - mm(weight, held_low)).astype(LOW)
            current[head] = last * held + mm_tn(tail, fresh)
            rows = pl.ds(block * BLOCK, BLOCK)
            outcome = mm(query_low, held_low) + mm(scores, fresh)
            os[head][rows, :] = outcome
            inv = lax.rsqrt(jnp.mean(outcome * outcome, axis=1, keepdims=True) + 1e-06)
            gate = sources[head][rows, 4 * KEYS : 6 * KEYS]
            mixed = outcome * inv * gain[...] * (gate * jax.nn.sigmoid(gate))
            outs[head][rows, :] = mixed.astype(LOW)
    state[0] = current[0]
    state[1] = current[1]
    branch[...] = (
        mm_nt(mixed_a[...], mix_mine[:, 7 * KEYS :])
        + mm_nt(mixed_b[...], mix_other[:, 7 * KEYS :])
    ).astype(LOW)


def mixer_backward_kernel(
    meta, params, mine, other, edge_a, edge_b, o_a, o_b, normed_in, d_branch, states, inverses,
    mix_mine, mix_other, taps, gain,
    d_mine, d_other, d_taps, d_gain, d_params, inward, d_norm_gain, state_grad, carry, dm_a, dm_b,
):
    step = pl.program_id(0)
    seq = pl.num_programs(0) - 1 - step
    groups = mine.shape[0] // BLOCK
    row, col = grid_of(BLOCK)

    @pl.when(step == 0)
    def _():
        state_grad[...] = jnp.zeros_like(state_grad)
        carry[...] = jnp.zeros_like(carry)
        d_taps[...] = jnp.zeros_like(d_taps)
        d_gain[...] = jnp.zeros_like(d_gain)
        d_params[...] = jnp.zeros_like(d_params)
        d_norm_gain[...] = jnp.zeros_like(d_norm_gain)

    dm_a[...] = mm(d_branch[...], mix_mine[:, 7 * KEYS :])
    dm_b[...] = mm(d_branch[...], mix_other[:, 7 * KEYS :])

    sources = (mine, other)
    edges = (edge_a, edge_b)
    os = (o_a, o_b)
    dms = (dm_a, dm_b)
    dsts = (d_mine, d_other)
    lower = jnp.where(row >= col, 1.0, 0.0)
    after = jnp.where(row > col, 1.0, 0.0)
    kept = {}
    gain_total = jnp.zeros((1, 2 * KEYS), F32)
    for head in range(2):
        source = sources[head]
        for block in range(groups):
            rows = pl.ds(block * BLOCK, BLOCK)
            keep = 1.0 - meta[1 + seq * groups + block].astype(F32)
            own = source[rows, 0 : 4 * KEYS]
            if block == 0:
                before = edges[head][:, 0 : 4 * KEYS]
            else:
                before = source[pl.ds(block * BLOCK - 8, 8), 0 : 4 * KEYS]
            shifted, conv = convolve(own, before * keep, taps[head])
            sig = jax.nn.sigmoid(conv)
            active = conv * sig
            slope = sig * (1.0 + conv * (1.0 - sig))
            query_unit, query_inv = unit(active[:, :KEYS])
            query = query_unit * KEYS ** (-0.5)
            keys, keys_inv = unit(active[:, KEYS : 2 * KEYS])
            values = active[:, 2 * KEYS :]
            decay_pre, log_decay, strength, cumlog, ratio = decay_of(
                source[rows, 6 * KEYS : 6 * KEYS + 2], params[head, 0], params[head, 1], row, col
            )
            gamma = jnp.exp(cumlog)
            last = cumlog[BLOCK - 1 :]
            tail_scale = jnp.exp(last - cumlog)
            both = mm_nt(jnp.concatenate([keys, query], axis=0), keys)
            near = jnp.where(row > col, ratio * both[:BLOCK], 0.0)
            scores = both[BLOCK:] * ratio
            inverse = inverses[block, head]
            held = states[block, head]
            weight = mm(inverse, (strength * gamma) * keys).astype(LOW)
            key_state = mm(keys, held)
            lacking = values - gamma * key_state
            fresh = mm(inverse, strength * lacking)
            outcome = os[head][rows, :]
            d_mixed = dms[head][rows, :]
            gate = source[rows, 4 * KEYS : 6 * KEYS]
            gate_sig = jax.nn.sigmoid(gate)
            gate_act = gate * gate_sig
            inv = lax.rsqrt(jnp.mean(outcome * outcome, axis=1, keepdims=True) + 1e-06)
            normed = outcome * inv
            weighted = d_mixed * gain[...]
            d_gate = weighted * normed * (gate_sig * (1.0 + gate * (1.0 - gate_sig)))
            dsts[head][rows, 4 * KEYS : 6 * KEYS] = d_gate.astype(LOW)
            gain_total = gain_total + jnp.sum(d_mixed * normed * gate_act, axis=0, keepdims=True)
            d_normed = weighted * gate_act
            d_out = inv * (d_normed - normed * jnp.mean(d_normed * normed, axis=1, keepdims=True))
            d_out_low = d_out.astype(LOW)
            part_fresh = mm_tn(scores, d_out_low)
            part_state = mm_tn(query * gamma, d_out_low)
            tail = keys * tail_scale
            kept[block, head] = dict(
                keep=keep, shifted=shifted, slope=slope, query_unit=query_unit, query_inv=query_inv,
                query=query, keys=keys, keys_inv=keys_inv, decay_pre=decay_pre, log_decay=log_decay,
                strength=strength, ratio=ratio, gamma=gamma, last=jnp.exp(last), tail=tail,
                tail_scale=tail_scale, near=near, scores=scores, inverse=inverse, held=held,
                weight=weight, key_state=key_state, lacking=lacking, fresh=fresh,
                d_out_low=d_out_low, part_fresh=part_fresh, part_state=part_state,
            )
    d_gain[...] += gain_total
    current = [state_grad[0], state_grad[1]]
    for block in reversed(range(groups)):
        for head in range(2):
            k = kept[block, head]
            k["ds"] = current[head]
            d_fresh = (k["part_fresh"] + mm(k["tail"], current[head])).astype(LOW)
            k["d_fresh"] = d_fresh
            below = k["last"] * current[head] + k["part_state"] - mm_tn(k["weight"], d_fresh)
            current[head] = below * k["keep"]
    state_grad[0] = current[0]
    state_grad[1] = current[1]
    for head in range(2):
        next_rows = carry[head]
        taps_here = taps[head]
        tap_sums = [jnp.zeros((1, 4 * KEYS), F32) for _ in range(4)]
        rate_sum = jnp.zeros((1, 1), F32)
        bias_sum = jnp.zeros((1, 1), F32)
        for block in reversed(range(groups)):
            rows = pl.ds(block * BLOCK, BLOCK)
            k = kept[block, head]
            keys, query, gamma, strength = k["keys"], k["query"], k["gamma"], k["strength"]
            fresh_low = k["fresh"].astype(LOW)
            ds_low = k["ds"].astype(LOW)
            d_fill = mm_tn(k["inverse"], k["d_fresh"])
            grams = mm_nt(jnp.concatenate([d_fill.astype(LOW), k["d_out_low"]], axis=0), fresh_low)
            d_below = jnp.where(row > col, -grams[:BLOCK], 0.0)
            d_scores = grams[BLOCK:]
            d_tail = mm_nt(fresh_low, ds_low)
            scaled = (strength * gamma) * d_fill
            through = mm_nt(jnp.concatenate([k["d_out_low"], scaled.astype(LOW)], axis=0), k["held"])
            d_qk = (d_scores * k["ratio"]).astype(LOW)
            d_kk = (strength * d_below * k["ratio"]).astype(LOW)
            pair = mm(jnp.concatenate([d_qk, d_kk], axis=0), keys)
            d_query = gamma * through[:BLOCK] + pair[:BLOCK]
            d_keys = (
                pair[BLOCK:]
                - through[BLOCK:]
                + k["tail_scale"] * d_tail
                + mm_tn(jnp.concatenate([d_qk, d_kk], axis=0), jnp.concatenate([query, keys], axis=0))
            )
            d_values = strength * d_fill
            d_strength = rowsum(d_fill * k["lacking"]) + rowsum(d_below * k["near"])
            spread_grad = d_scores * k["scores"] + strength * d_below * k["near"]
            tail_part = rowsum(d_tail * k["tail"])
            d_cum = gamma * rowsum(query * through[:BLOCK]) - rowsum(scaled * k["key_state"]) - tail_part
            at_last = jnp.sum(tail_part, axis=0, keepdims=True) + k["last"] * jnp.sum(
                rowsum(k["ds"] * k["held"].astype(F32)), axis=0, keepdims=True
            )
            place = lax.broadcasted_iota(jnp.int32, (BLOCK, 1), 0)
            d_cum = d_cum + jnp.where(place == BLOCK - 1, at_last, 0.0)
            spread_grad = spread_grad + jnp.where(col == 0, d_cum, 0.0)
            d_log = rowsum(exact(lower, spread_grad, ((0,), (0,))) * after)
            d_log = d_log + jnp.where(place == 0, jnp.sum(d_cum, axis=0, keepdims=True), 0.0)
            d_decay = d_log * (-params[head, 0]) * jax.nn.sigmoid(k["decay_pre"])
            rate_sum = rate_sum + jnp.sum(d_log * k["log_decay"], axis=0, keepdims=True)
            bias_sum = bias_sum + jnp.sum(d_decay, axis=0, keepdims=True)
            d_write = d_strength * strength * (1.0 - strength)
            lanes = lax.broadcasted_iota(jnp.int32, (BLOCK, KEYS), 1)
            dsts[head][rows, 6 * KEYS : 7 * KEYS] = (
                jnp.where(lanes == 0, d_decay, 0.0) + jnp.where(lanes == 1, d_write, 0.0)
            ).astype(LOW)
            d_query = d_query * KEYS ** (-0.5)
            unit_q = k["query_unit"]
            d_active = jnp.concatenate(
                [
                    k["query_inv"] * (d_query - unit_q * rowsum(unit_q * d_query)),
                    k["keys_inv"] * (d_keys - keys * rowsum(keys * d_keys)),
                    d_values,
                ],
                axis=1,
            )
            d_conv = d_active * k["slope"]
            padded = jnp.concatenate([d_conv, next_rows], axis=0)
            d_own = taps_here[0:1] * d_conv
            tap_sums[0] = tap_sums[0] + jnp.sum(d_conv * k["shifted"][0], axis=0, keepdims=True)
            for lag in range(1, 4):
                moved = pltpu.roll(padded, BLOCK + 8 - lag, 0)[:BLOCK]
                d_own = d_own + taps_here[lag : lag + 1] * moved
                tap_sums[lag] = tap_sums[lag] + jnp.sum(
                    d_conv * k["shifted"][lag], axis=0, keepdims=True
                )
            dsts[head][rows, 0 : 4 * KEYS] = d_own.astype(LOW)
            next_rows = d_conv[0:8] * k["keep"]
        carry[head] = next_rows
        for lag in range(4):
            d_taps[head, lag : lag + 1, :] += tap_sums[lag]
        lane = lax.broadcasted_iota(jnp.int32, (1, KEYS), 1)
        d_params[head : head + 1, :] += jnp.where(lane == 0, rate_sum, 0.0) + jnp.where(
            lane == 1, bias_sum, 0.0
        )
    back = mm_nt(d_mine[...], mix_mine[:, : 7 * KEYS]) + mm_nt(d_other[...], mix_other[:, : 7 * KEYS])
    inward[...] = back.astype(LOW)
    d_norm_gain[...] += jnp.sum(back * normed_in[...].astype(F32), axis=0, keepdims=True)


def ffn_forward_kernel(rows, mine, other, u_a, u_b, act_a, act_b, out):
    half = mine.shape[1] // 3
    total = None
    for weight, u_out, act in ((mine, u_a, act_a), (other, u_b, act_b)):
        u = mm(rows[...], weight[:, : 2 * half])
        u_out[...] = u
        gate = u[:, :half]
        active = (gate * jax.nn.sigmoid(gate) * u[:, half:]).astype(LOW)
        act[...] = active
        piece = mm_nt(active, weight[:, 2 * half :])
        total = piece if total is None else total + piece
    out[...] = total.astype(LOW)


def ffn_backward_kernel(grad, u_a, u_b, mine, other, d_a, d_b, out):
    half = mine.shape[1] // 3
    total = None
    for weight, u_in, d_out in ((mine, u_a, d_a), (other, u_b, d_b)):
        d_active = mm(grad[...], weight[:, 2 * half :])
        gate, lift = u_in[:, :half], u_in[:, half:]
        sig = jax.nn.sigmoid(gate)
        d_gate = (d_active * lift * (sig * (1.0 + gate * (1.0 - sig)))).astype(LOW)
        d_lift = (d_active * (gate * sig)).astype(LOW)
        d_out[:, :half] = d_gate
        d_out[:, half:] = d_lift
        piece = mm_nt(d_gate, weight[:, :half]) + mm_nt(d_lift, weight[:, half : 2 * half])
        total = piece if total is None else total + piece
    out[...] = total.astype(LOW)


def ffn_forward(rows, weights):
    count, width = rows.shape
    half = weights[0].shape[1] // 3
    return pl.pallas_call(
        ffn_forward_kernel,
        out_shape=[
            jax.ShapeDtypeStruct((count, 2 * half), F32),
            jax.ShapeDtypeStruct((count, 2 * half), F32),
            jax.ShapeDtypeStruct((count, half), LOW),
            jax.ShapeDtypeStruct((count, half), LOW),
            jax.ShapeDtypeStruct((count, width), LOW),
        ],
        compiler_params=pltpu.CompilerParams(vmem_limit_bytes=VMEM_LIMIT),
        name="ffn_forward",
    )(rows, *weights)


def ffn_backward(grad, pair, weights):
    count, width = grad.shape
    half = weights[0].shape[1] // 3
    return pl.pallas_call(
        ffn_backward_kernel,
        out_shape=[
            jax.ShapeDtypeStruct((count, 2 * half), LOW),
            jax.ShapeDtypeStruct((count, 2 * half), LOW),
            jax.ShapeDtypeStruct((count, width), LOW),
        ],
        compiler_params=pltpu.CompilerParams(vmem_limit_bytes=VMEM_LIMIT),
        name="ffn_backward",
    )(grad, *pair, *weights)


def whole(array):
    return pl.BlockSpec(array.shape, lambda step, meta: (0,) * array.ndim)


def mixer_forward(meta, params, normed, weights, taps, gain, parts):
    rows, width = normed.shape
    wide = 7 * KEYS
    group = rows // parts
    per = group // BLOCK

    def place(step, meta):
        return (step ^ meta[0], 0)

    def stacked(step, meta):
        return (step, 0, 0, 0)

    vals = 2 * KEYS
    row_spec = pl.BlockSpec((group, vals), place)
    wide_spec = pl.BlockSpec((group, wide), place)
    full_spec = pl.BlockSpec((group, width), place)
    return pl.pallas_call(
        mixer_forward_kernel,
        grid_spec=pltpu.PrefetchScalarGridSpec(
            num_scalar_prefetch=1,
            grid=(parts,),
            in_specs=[
                pl.BlockSpec(memory_space=pltpu.SMEM),
                full_spec,
                *[whole(weight) for weight in weights],
                whole(taps),
                whole(gain),
            ],
            out_specs=[
                wide_spec,
                wide_spec,
                row_spec,
                row_spec,
                row_spec,
                row_spec,
                pl.BlockSpec((per, 2, KEYS, vals), stacked),
                pl.BlockSpec((per, 2, BLOCK, BLOCK), stacked),
                full_spec,
            ],
            scratch_shapes=[pltpu.VMEM((2, KEYS, vals), F32), pltpu.VMEM((2, 8, 4 * KEYS), F32)],
        ),
        out_shape=[
            jax.ShapeDtypeStruct((rows, wide), F32),
            jax.ShapeDtypeStruct((rows, wide), F32),
            jax.ShapeDtypeStruct((rows, vals), LOW),
            jax.ShapeDtypeStruct((rows, vals), LOW),
            jax.ShapeDtypeStruct((rows, vals), F32),
            jax.ShapeDtypeStruct((rows, vals), F32),
            jax.ShapeDtypeStruct((rows // BLOCK, 2, KEYS, vals), LOW),
            jax.ShapeDtypeStruct((rows // BLOCK, 2, BLOCK, BLOCK), LOW),
            jax.ShapeDtypeStruct((rows, width), LOW),
        ],
        compiler_params=pltpu.CompilerParams(vmem_limit_bytes=VMEM_LIMIT),
        name="mixer_forward",
    )(meta, params, normed, *weights, taps, gain)


def mixer_backward(meta, params, saved, normed, d_branch, weights, taps, gain, parts):
    mine, other, o_a, o_b, states, inverses = saved
    rows, width = normed.shape
    wide = mine.shape[1]
    group = rows // parts
    per = group // BLOCK

    def place(step, meta):
        return ((parts - 1 - step) ^ meta[0], 0)

    def edge(step, meta):
        return ((jnp.maximum(parts - 2 - step, 0) ^ meta[0]) * (group // 8) + group // 8 - 1, 0)

    def stacked(step, meta):
        return (parts - 1 - step, 0, 0, 0)

    vals = 2 * KEYS
    row_spec = pl.BlockSpec((group, vals), place)
    wide_spec = pl.BlockSpec((group, wide), place)
    full_spec = pl.BlockSpec((group, width), place)
    edge_spec = pl.BlockSpec((8, wide), edge)
    return pl.pallas_call(
        mixer_backward_kernel,
        grid_spec=pltpu.PrefetchScalarGridSpec(
            num_scalar_prefetch=1,
            grid=(parts,),
            in_specs=[
                pl.BlockSpec(memory_space=pltpu.SMEM),
                wide_spec,
                wide_spec,
                edge_spec,
                edge_spec,
                row_spec,
                row_spec,
                full_spec,
                full_spec,
                pl.BlockSpec((per, 2, KEYS, vals), stacked),
                pl.BlockSpec((per, 2, BLOCK, BLOCK), stacked),
                *[whole(weight) for weight in weights],
                whole(taps),
                whole(gain),
            ],
            out_specs=[
                wide_spec,
                wide_spec,
                whole(taps),
                whole(gain),
                pl.BlockSpec((2, KEYS), lambda step, meta: (0, 0)),
                full_spec,
                pl.BlockSpec((1, width), lambda step, meta: (0, 0)),
            ],
            scratch_shapes=[
                pltpu.VMEM((2, KEYS, vals), F32),
                pltpu.VMEM((2, 8, 4 * KEYS), F32),
                pltpu.VMEM((group, vals), F32),
                pltpu.VMEM((group, vals), F32),
            ],
        ),
        out_shape=[
            jax.ShapeDtypeStruct((rows, wide), LOW),
            jax.ShapeDtypeStruct((rows, wide), LOW),
            jax.ShapeDtypeStruct(taps.shape, F32),
            jax.ShapeDtypeStruct(gain.shape, F32),
            jax.ShapeDtypeStruct((2, KEYS), F32),
            jax.ShapeDtypeStruct((rows, width), LOW),
            jax.ShapeDtypeStruct((1, width), F32),
        ],
        compiler_params=pltpu.CompilerParams(vmem_limit_bytes=VMEM_LIMIT),
        name="mixer_backward",
    )(
        meta, params, mine, other, mine, other, o_a, o_b, normed, d_branch, states, inverses,
        *weights, taps, gain,
    )


def swap_section(array):
    return lax.ppermute(array, "section", [(0, 1), (1, 0)])


def send_by(array, offset):
    peers = lax.axis_size("tensor")
    return lax.ppermute(array, "tensor", [(i, i ^ offset) for i in range(peers)])


def spread_rows(values):
    peers = lax.axis_size("tensor")
    return [values] + [send_by(values, k) for k in range(1, peers)]


def collect_rows(parts):
    total = parts[0].astype(F32)
    for k in range(1, len(parts)):
        total = total + send_by(parts[k].astype(LOW), k).astype(F32)
    return total


def nn(left, right):
    return jnp.dot(left, right, preferred_element_type=F32)


def nt(left, right):
    return lax.dot_general(left, right, (((1,), (1,)), ((), ())), preferred_element_type=F32)


def tn(left, right):
    return lax.dot_general(left, right, (((0,), (0,)), ((), ())), preferred_element_type=F32)


def norm_forward(hidden, gain):
    inv = lax.rsqrt(jnp.mean(hidden * hidden, axis=-1, keepdims=True) + 1e-06)
    return (hidden * inv * gain).astype(LOW), inv


def norm_backward(hidden, inv, gain, grad):
    normed = hidden * inv
    weighted = grad * gain
    back = inv * (weighted - normed * jnp.mean(weighted * normed, axis=-1, keepdims=True))
    return back, jnp.sum(grad * normed, axis=0)


def layout(lengths_row, buffer):
    ends = jnp.cumsum(lengths_row, dtype=jnp.int32)
    token = jnp.arange(buffer, dtype=jnp.int32)
    start = jnp.max(jnp.where(ends[None, :] <= token[:, None], ends[None, :], 0), axis=1)
    live = (token < ends[-1]).astype(F32)
    reset = ((token - start)[::BLOCK] == 0).astype(jnp.int32)
    return live, reset


def split_rows(array, count):
    size = array.shape[0] // count
    return [array[k * size : (k + 1) * size] for k in range(count)]


def layer_forward(hidden, weights, gains, small, meta, live, between, last):
    mix_weights = weights
    params, taps, gain_out = small
    peers = lax.axis_size("tensor")
    normed, inv_one = norm_forward(hidden, gains[0])
    normed_all = jnp.concatenate(spread_rows(normed), axis=0)
    if last is not None:
        normed_all, last = lax.optimization_barrier((normed_all, last))
        last = spread_rows(last)
    mine, other, mixed_a, mixed_b, o_a, o_b, states, inverses, branch = mixer_forward(
        meta, params, normed_all, mix_weights, taps, gain_out, peers
    )
    ffn_weights = between[0](branch)
    if last is not None:
        branch, last = lax.optimization_barrier((branch, last))
    branch = collect_rows(split_rows(branch, peers))
    after = hidden + live * branch
    normed_two, inv_two = norm_forward(after, gains[1])
    normed_two_all = spread_rows(normed_two)
    ups, actives, ffn = [], [], []
    for place, chunk in enumerate(normed_two_all):
        if place:
            chunk, ffn[-1] = lax.optimization_barrier((chunk, ffn[-1]))
        u_a, u_b, act_a, act_b, partial = ffn_forward(chunk, ffn_weights)
        ups.append((u_a, u_b))
        actives.append((act_a, act_b))
        ffn.append(partial)
    between[1](ffn[-1])
    kept = (
        hidden, inv_one, normed_all, mine, other, o_a, o_b, states, inverses, mixed_a, mixed_b,
        after, inv_two, normed_two_all, ups, actives,
    )
    return ffn, kept, last, (mix_weights, ffn_weights)


def finish_forward(after, live, ffn):
    return (after + live * collect_rows(ffn)).astype(LOW)


def share(mine, other):
    got = swap_section(other.astype(LOW))
    return (mine + got.astype(F32)).astype(LOW)


def scatter(total):
    return lax.psum_scatter(total, "dp", scatter_dimension=0, tiled=True)


def exchange_sum(array, axis):
    peers = lax.axis_size(axis)
    offset = 1
    while offset < peers:
        array = array + lax.ppermute(array, axis, [(i, i ^ offset) for i in range(peers)])
        offset *= 2
    return array


def layer_backward(grad, kept, weights, gains, small, meta, live, ffn_grads, waiting, beside, final):
    mix_weights, ffn_weights = weights
    params, taps, gain_out = small
    (
        hidden, inv_one, normed_all, mine, other, o_a, o_b, states, inverses, mixed_a, mixed_b,
        after, inv_two, normed_two_all, ups, actives,
    ) = kept
    peers = lax.axis_size("tensor")
    if ffn_grads is None:
        ffn_grads = spread_rows((live * grad).astype(LOW))
    d_ups, back = ([], []), []
    for chunk, pair in zip(ffn_grads, ups):
        d_a, d_b, partial = ffn_backward(chunk, pair, ffn_weights)
        d_ups[0].append(d_a)
        d_ups[1].append(d_b)
        back.append(partial)
    back_two = collect_rows(back)
    two_all = jnp.concatenate(normed_two_all, axis=0)
    ffn_all = jnp.concatenate(ffn_grads, axis=0)
    ffn_parts = []
    for side in range(2):
        d_up_all = jnp.concatenate(d_ups[side], axis=0)
        active_all = jnp.concatenate([pair[side] for pair in actives], axis=0)
        ffn_parts.append((tn(two_all, d_up_all), tn(ffn_all, active_all)))
    ffn_total = share(*[jnp.concatenate(part, axis=1) for part in ffn_parts])
    back, gain_two_grad = norm_backward(after, inv_two, gains[1], back_two)
    grad_after = grad + back
    branch_all = jnp.concatenate(spread_rows((live * grad_after).astype(LOW)), axis=0)
    out_total = share(tn(branch_all, mixed_a), tn(branch_all, mixed_b))
    early = jnp.concatenate([ffn_total, out_total], axis=1)
    early, branch_all, waiting = lax.optimization_barrier((early, branch_all, waiting))
    early_owned = scatter(early)
    d_mine, d_other, d_taps, d_gain, d_params, inward, gain_one_grad = mixer_backward(
        meta, params, (mine, other, o_a, o_b, states, inverses), normed_all, branch_all,
        mix_weights, taps, gain_out, peers,
    )
    waiting = beside(waiting)
    inward, waiting = lax.optimization_barrier((inward, waiting))
    mix_total = share(tn(normed_all, d_mine[:, : 6 * KEYS]), tn(normed_all, d_other[:, : 6 * KEYS]))
    if final:
        inward, mix_total = lax.optimization_barrier((inward, mix_total))
    back_one = collect_rows(split_rows(inward, peers))
    early_owned, mix_total = lax.optimization_barrier((early_owned, mix_total))
    mix_owned = scatter(mix_total)
    pairs = jnp.concatenate([d[:, 6 * KEYS : 6 * KEYS + 2] for d in (d_mine, d_other)], axis=1)
    decay_grad = tn(pairs, normed_all)
    gain_one_grad = gain_one_grad[0] / gains[0]
    back, _ = norm_backward(hidden, inv_one, gains[0], back_one)
    return (
        grad_after + back,
        [early_owned, mix_owned],
        (jnp.stack([gain_one_grad, gain_two_grad]), *lax.optimization_barrier((d_taps, d_params, d_gain, decay_grad, mix_total))[:4]),
        waiting,
    )


def on_device(
    inputs, lengths, norm_gain, w_query, w_key, w_value, w_gate, w_decay, conv_weight, head_rate,
    head_bias, out_gain, w_out, w_updown, w_down, cotangent,
):
    section = lax.axis_index("section")
    layers = lax.axis_size("section")
    first = section == 0
    part = lax.axis_index("tensor")
    rows_here = inputs.shape[1]
    buffer = rows_here * lax.axis_size("tensor")
    ff = w_down.shape[1]
    half = ff // 2
    wide = -(-half // KEYS) * KEYS
    vals = 2 * KEYS

    def zeros(count):
        return jnp.zeros((w_query.shape[1], count), LOW)

    def half_mix(h):
        return jnp.concatenate(
            [
                w_query[0][:, h * KEYS : (h + 1) * KEYS],
                w_key[0][:, h * KEYS : (h + 1) * KEYS],
                w_value[0][:, h * vals : (h + 1) * vals],
                w_gate[0][:, h * vals : (h + 1) * vals],
                w_decay[0][:, h * 2 : (h + 1) * 2],
                zeros(KEYS - 2),
                w_out[0][h * vals : (h + 1) * vals].T,
            ],
            axis=1,
        )

    def half_ffn(h):
        hidden_part = slice(h * half, (h + 1) * half)
        return jnp.concatenate(
            [
                w_updown[0][:, 0, hidden_part],
                zeros(wide - half),
                w_updown[0][:, 1, hidden_part],
                zeros(wide - half),
                w_down[0][hidden_part].T,
                zeros(wide - half),
            ],
            axis=1,
        )

    def both_layers(halves):
        keep = jnp.where(first, halves[0], halves[1])
        got = swap_section(jnp.where(first, halves[1], halves[0]))
        return jnp.where(first, keep, got), jnp.where(first, got, keep)

    mix_shards = both_layers((half_mix(0), half_mix(1)))
    ffn_shards = both_layers((half_ffn(0), half_ffn(1)))

    def gather(shard, *before):
        if before:
            shard, *before = lax.optimization_barrier((shard, *before))
        full = lax.all_gather(shard, "dp", axis=0, tiled=True)
        return (full, *before)

    def of_all(array):
        got = swap_section(array)
        return jnp.concatenate(
            [jnp.where(first, array, got), jnp.where(first, got, array)], axis=0
        )

    gains_all = of_all(norm_gain)
    sizes = (conv_weight.size, head_rate.size, head_bias.size, out_gain.size)
    packed = of_all(
        jnp.concatenate(
            [conv_weight.reshape(-1), head_rate.reshape(-1), head_bias.reshape(-1), out_gain.reshape(-1)]
        )[None]
    )
    edges = [0]
    for size in sizes:
        edges.append(edges[-1] + size)
    heads = conv_weight.shape[2]
    places = [part * 2 + section, part * 2 + 1 - section]
    smalls = []
    for layer in range(2):
        conv, rate, bias, gain_out = (packed[layer, a:b] for a, b in zip(edges[:-1], edges[1:]))
        conv = conv.reshape(conv_weight.shape[1:])
        taps = jnp.concatenate(
            [lax.dynamic_slice_in_dim(conv, p, 1, 1) for p in places], axis=1
        ).transpose(1, 0, 2)
        scale = jnp.stack([jnp.exp(rate), bias], axis=1)
        params = jnp.concatenate([lax.dynamic_slice_in_dim(scale, p, 1, 0) for p in places], axis=0)
        smalls.append((params, taps, gain_out[None]))

    lengths_row = lax.dynamic_index_in_dim(lengths[:, 0], section, 0, keepdims=False)
    live_all, reset = layout(lengths_row, buffer)
    live = lax.dynamic_slice_in_dim(live_all, part * rows_here, rows_here)[:, None]
    meta = jnp.concatenate([part[None].astype(jnp.int32), reset])

    def own_micro(array):
        return lax.dynamic_index_in_dim(array, section, 0, keepdims=False).astype(F32)

    hidden = own_micro(inputs)
    (mix_full,) = gather(mix_shards[0])
    ffn_full, mix_full = gather(ffn_shards[0], mix_full)
    mix_pair = (mix_full, swap_section(mix_full))
    held = {}

    def first_mixed(branch):
        held["mix"], full, _ = gather(mix_shards[1], ffn_full, branch)
        return full, swap_section(full)

    def first_done(partial):
        held["ffn"], held["mix"], _ = gather(ffn_shards[1], held["mix"], partial)

    def second_mixed(branch):
        return held["ffn"], swap_section(held["ffn"])

    def second_done(partial):
        pass

    ffn, saved, _, weights_one = layer_forward(
        hidden, mix_pair, gains_all[0], smalls[0], meta, live, (first_mixed, first_done), None
    )
    kept = [saved]
    hidden = finish_forward(saved[11], live, ffn).astype(F32)
    mix_pair = (held["mix"], swap_section(held["mix"]))
    ffn_last, saved, spread, weights_two = layer_forward(
        hidden, mix_pair, gains_all[1], smalls[1], meta, live, (second_mixed, second_done),
        (live * own_micro(cotangent)).astype(LOW),
    )
    kept.append(saved)
    weights = [weights_one, weights_two]

    grad = own_micro(cotangent)
    owned, small_grads = [None, None], [None, None]
    for layer in (1, 0):
        waiting = ffn_last if layer == 1 else owned[1]
        grad, owned[layer], small_grads[layer], waiting = layer_backward(
            grad, kept[layer], weights[layer], gains_all[layer], smalls[layer], meta, live,
            spread if layer == 1 else None, waiting,
            (lambda parts: finish_forward(kept[1][11], live, parts)) if layer == 1 else (lambda x: x),
            layer == 0,
        )
        if layer == 0:
            owned[1] = waiting
        else:
            result_low = waiting
        grad_low = grad.astype(LOW)
        grad = grad_low.astype(F32)

    halves = []
    for kind in range(2):
        keep = jnp.where(first, owned[0][kind], owned[1][kind])
        got = swap_section(jnp.where(first, owned[1][kind], owned[0][kind]))
        halves.append(
            (
                jnp.where(first, keep, got).astype(F32),
                jnp.where(first, got, keep).astype(F32),
            )
        )
    early_pair, mix_pair = halves

    def columns(pair, start, size):
        return jnp.concatenate([side[:, start : start + size] for side in pair], axis=1)

    grad_updown = jnp.stack([columns(early_pair, 0, half), columns(early_pair, wide, half)], axis=1)
    grad_down = columns(early_pair, 2 * wide, half).T
    grad_out = columns(early_pair, 3 * wide, vals).T
    grad_query = columns(mix_pair, 0, KEYS)
    grad_key = columns(mix_pair, KEYS, KEYS)
    grad_value = columns(mix_pair, 2 * KEYS, vals)
    grad_gate = columns(mix_pair, vals + 2 * KEYS, vals)

    pairs = jnp.stack([small_grads[layer][4] for layer in range(2)])
    pairs = exchange_sum(pairs[:, :2] + swap_section(pairs[:, 2:]), "dp")
    pairs = lax.dynamic_slice_in_dim(
        pairs, lax.axis_index("dp") * w_query.shape[1], w_query.shape[1], 2
    )
    keep = jnp.where(first, pairs[0], pairs[1])
    got = swap_section(jnp.where(first, pairs[1], pairs[0]))
    grad_decay = jnp.concatenate([jnp.where(first, keep, got), jnp.where(first, got, keep)], axis=0).T

    flat = []
    for layer in range(2):
        gain_grads, d_taps, d_params, d_gain, _ = small_grads[layer]
        conv_full = jnp.zeros(conv_weight.shape[1:], F32)
        pair_full = jnp.zeros((heads, 2), F32)
        for side, p in enumerate(places):
            conv_full = lax.dynamic_update_slice_in_dim(conv_full, d_taps[side][:, None, :], p, 1)
            pair_full = lax.dynamic_update_slice_in_dim(pair_full, d_params[side : side + 1, :2], p, 0)
        flat.append(
            jnp.concatenate(
                [
                    conv_full.reshape(-1), pair_full[:, 0], pair_full[:, 1], d_gain.reshape(-1),
                    gain_grads.reshape(-1),
                ]
            )
        )
    got = swap_section(jnp.where(first, flat[1], flat[0]))
    own = jnp.where(first, flat[0], flat[1]) + got
    own = exchange_sum(exchange_sum(own, "tensor"), "dp")
    pieces = [own[a:b] for a, b in zip(edges[:-1], edges[1:])]
    return (
        result_low[None],
        grad_low[None],
        own[edges[-1] :].reshape(norm_gain.shape),
        grad_query[None],
        grad_key[None],
        grad_value[None],
        grad_gate[None],
        grad_decay[None],
        pieces[0].reshape(conv_weight.shape),
        pieces[1].reshape(head_rate.shape),
        pieces[2].reshape(head_bias.shape),
        pieces[3].reshape(out_gain.shape),
        grad_out[None],
        grad_updown[None],
        grad_down[None],
    )


def solution(mesh):
    in_specs = (
        P(None, ("dp", "tensor"), None),
        P(None, "dp", None),
        P("section", None, None),
        P("section", "dp", "tensor"),
        P("section", "dp", "tensor"),
        P("section", "dp", "tensor"),
        P("section", "dp", "tensor"),
        P("section", "dp", "tensor"),
        P("section", None, None, None),
        P("section", None),
        P("section", None),
        P("section", None),
        P("section", "tensor", "dp"),
        P("section", "dp", None, "tensor"),
        P("section", "tensor", "dp"),
        P(None, ("dp", "tensor"), None),
    )
    out_specs = (
        P("section", ("dp", "tensor"), None),
        P("section", ("dp", "tensor"), None),
        P("section", None, None),
        P("section", "dp", "tensor"),
        P("section", "dp", "tensor"),
        P("section", "dp", "tensor"),
        P("section", "dp", "tensor"),
        P("section", "dp", "tensor"),
        P("section", None, None, None),
        P("section", None),
        P("section", None),
        P("section", None),
        P("section", "tensor", "dp"),
        P("section", "dp", None, "tensor"),
        P("section", "tensor", "dp"),
    )
    return jax.shard_map(
        on_device, mesh=mesh, in_specs=in_specs, out_specs=out_specs, check_vma=False
    )
```

```python
import jax
import jax.numpy as jnp
from jax import lax
from jax.experimental import pallas as pl
from jax.experimental.pallas import tpu as pltpu
from jax.sharding import PartitionSpec as P

KEYS = 128
BLOCK = 64
F32 = jnp.float32
LOW = jnp.bfloat16
WIDTH = 8
MIXER_VMEM = 56 * 1024 * 1024
FFN_VMEM = 14 * 1024 * 1024


def _dot(left, right, dims):
    return lax.dot_general(
        left.astype(LOW), right.astype(LOW), (dims, ((), ())), preferred_element_type=F32
    )


def mm(left, right):
    return _dot(left, right, ((1,), (0,)))


def mm_nt(left, right):
    return _dot(left, right, ((1,), (1,)))


def mm_tn(left, right):
    return _dot(left, right, ((0,), (0,)))


def exact(left, right, dims=((1,), (0,))):
    return lax.dot_general(
        left, right, (dims, ((), ())), precision=lax.Precision.HIGHEST, preferred_element_type=F32
    )


def mm_split(left, right):
    left_high = left.astype(LOW)
    right_high = right.astype(LOW)
    left_low = (left - left_high.astype(F32)).astype(LOW)
    right_low = (right - right_high.astype(F32)).astype(LOW)
    return mm(left_high, right_high) + (mm(left_high, right_low) + mm(left_low, right_high))


def grid_of(size):
    row = lax.broadcasted_iota(jnp.int32, (size, size), 0)
    col = lax.broadcasted_iota(jnp.int32, (size, size), 1)
    return row, col


def rowsum(array):
    return jnp.sum(array, axis=1, keepdims=True)


def side_by_side(steps, width):
    for first in range(0, len(steps), width):
        running = steps[first : first + width]
        while running:
            running = [step for step in running if next(step, running) is not running]


def unit_lower_inverses(belows, row, col):
    ones = jnp.where(row == col, 1.0, 0.0)
    near = row // 2 == col // 2
    inverses = [ones - jnp.where(near, below, 0.0) for below in belows]
    half = 2
    while half < BLOCK:
        span = 2 * half
        part = (row // span == col // span) & (row % span >= half) & (col % span < half)
        pieces = [mm_split(jnp.where(part, b, 0.0), i) for b, i in zip(belows, inverses)]
        inverses = [i - mm_split(i, p) for p, i in zip(pieces, inverses)]
        half = span
    return inverses


def convolve(own, before, taps):
    padded = jnp.concatenate([before, own], axis=0)
    shifted = [own]
    total = taps[0:1] * own
    for lag in range(1, taps.shape[0]):
        moved = pltpu.roll(padded, lag, 0)[8:]
        shifted.append(moved)
        total = total + taps[lag : lag + 1] * moved
    return shifted, total


def decay_of(pair, rate_exp, bias, row, col):
    shifted = pair[:, 0:1] + bias
    soft = jnp.maximum(shifted, 0.0) + jnp.log1p(jnp.exp(-jnp.abs(shifted)))
    log_decay = -rate_exp * soft
    strength = jax.nn.sigmoid(pair[:, 1:2])
    lower = jnp.where(row >= col, 1.0, 0.0)
    after = jnp.where(row > col, 1.0, 0.0)
    spread = exact(lower, log_decay * after)
    cumlog = spread[:, 0:1] + log_decay[0:1]
    ratio = jnp.where(row >= col, jnp.exp(spread), 0.0)
    return shifted, log_decay, strength, cumlog, ratio


def unit(array, scale=1.0):
    inv = lax.rsqrt(rowsum(array * array) + 1e-06)
    return array * inv, inv * scale


def mixer_forward_kernel(
    meta, params, normed, mix_mine, mix_other, taps, gain,
    mine, other, mixed_a, mixed_b, o_a, o_b, states, inverses, branch, state, carry,
):
    step = pl.program_id(0)
    groups = mine.shape[0] // BLOCK
    row, col = grid_of(BLOCK)

    @pl.when(step == 0)
    def _():
        state[...] = jnp.zeros_like(state)
        carry[...] = jnp.zeros_like(carry)

    mine[...] = mm(normed[...], mix_mine[:, : 7 * KEYS])
    other[...] = mm(normed[...], mix_other[:, : 7 * KEYS])
    sources = (mine, other)
    outs = (mixed_a, mixed_b)
    os = (o_a, o_b)
    prepared = {}

    def prepare(head, block):
        source = sources[head]
        rows = pl.ds(block * BLOCK, BLOCK)
        keep = 1.0 - meta[1 + step * groups + block].astype(F32)
        own = source[rows, 0 : 4 * KEYS]
        if block == 0:
            before = carry[head]
        else:
            before = source[pl.ds(block * BLOCK - 8, 8), 0 : 4 * KEYS]
        _, conv = convolve(own, before * keep, taps[head])
        active = conv * jax.nn.sigmoid(conv)
        yield
        query, _ = unit(active[:, :KEYS])
        query = query * KEYS ** (-0.5)
        keys, _ = unit(active[:, KEYS : 2 * KEYS])
        values = active[:, 2 * KEYS :]
        yield
        _, _, strength, cumlog, ratio = decay_of(
            source[rows, 6 * KEYS : 6 * KEYS + 2], params[head, 0], params[head, 1], row, col
        )
        yield
        gamma = jnp.exp(cumlog)
        last = cumlog[BLOCK - 1 :]
        both = mm_nt(jnp.concatenate([keys, query], axis=0), keys)
        yield
        below = jnp.where(row > col, strength * ratio * both[:BLOCK], 0.0)
        scores = (both[BLOCK:] * ratio).astype(LOW)
        tail = (keys * jnp.exp(last - cumlog)).astype(LOW)
        prepared[block, head] = (
            below,
            ((strength * gamma) * keys).astype(LOW),
            (strength * values).astype(LOW),
            scores,
            tail,
            (query * gamma).astype(LOW),
            jnp.exp(last),
            keep,
        )

    places = [(block, head) for block in range(groups) for head in range(2)]
    side_by_side([prepare(head, block) for block, head in places], WIDTH)
    for head in range(2):
        carry[head] = sources[head][pl.ds(groups * BLOCK - 8, 8), 0 : 4 * KEYS]
    order = list(prepared)
    solved = unit_lower_inverses([prepared[place][0] for place in order], row, col)
    for place, inverse in zip(order, solved):
        inverse_low = inverse.astype(LOW)
        inverses[place[0], place[1]] = inverse_low
        _, scaled_keys, scaled_values, *rest = prepared[place]
        weight = mm(inverse_low, scaled_keys).astype(LOW)
        prepared[place] = (weight, mm(inverse_low, scaled_values), *rest)
    current = [state[0], state[1]]
    for block in range(groups):
        for head in range(2):
            weight, update, scores, tail, query_low, last, keep = prepared[block, head]
            held = current[head] * keep
            held_low = held.astype(LOW)
            states[block, head] = held_low
            fresh = (update - mm(weight, held_low)).astype(LOW)
            current[head] = last * held + mm_tn(tail, fresh)
            rows = pl.ds(block * BLOCK, BLOCK)
            outcome = mm(query_low, held_low) + mm(scores, fresh)
            os[head][rows, :] = outcome
            inv = lax.rsqrt(jnp.mean(outcome * outcome, axis=1, keepdims=True) + 1e-06)
            gate = sources[head][rows, 4 * KEYS : 6 * KEYS]
            mixed = outcome * inv * gain[...] * (gate * jax.nn.sigmoid(gate))
            outs[head][rows, :] = mixed.astype(LOW)
    state[0] = current[0]
    state[1] = current[1]
    branch[...] = (
        mm_nt(mixed_a[...], mix_mine[:, 7 * KEYS :])
        + mm_nt(mixed_b[...], mix_other[:, 7 * KEYS :])
    ).astype(LOW)


def mixer_backward_kernel(
    meta, params, mine, other, edge_a, edge_b, o_a, o_b, normed_in, d_branch, states, inverses,
    mix_mine, mix_other, taps, gain,
    d_mine, d_other, d_taps, d_gain, d_params, inward, d_norm_gain, state_grad, carry, dm_a, dm_b,
):
    step = pl.program_id(0)
    seq = pl.num_programs(0) - 1 - step
    groups = mine.shape[0] // BLOCK
    row, col = grid_of(BLOCK)

    @pl.when(step == 0)
    def _():
        state_grad[...] = jnp.zeros_like(state_grad)
        carry[...] = jnp.zeros_like(carry)
        d_taps[...] = jnp.zeros_like(d_taps)
        d_gain[...] = jnp.zeros_like(d_gain)
        d_params[...] = jnp.zeros_like(d_params)
        d_norm_gain[...] = jnp.zeros_like(d_norm_gain)

    dm_a[...] = mm(d_branch[...], mix_mine[:, 7 * KEYS :])
    dm_b[...] = mm(d_branch[...], mix_other[:, 7 * KEYS :])

    sources = (mine, other)
    edges = (edge_a, edge_b)
    os = (o_a, o_b)
    dms = (dm_a, dm_b)
    dsts = (d_mine, d_other)
    lower = jnp.where(row >= col, 1.0, 0.0)
    after = jnp.where(row > col, 1.0, 0.0)
    kept = {}
    gain_parts = []
    places = [(block, head) for block in range(groups) for head in range(2)]

    def recompute(head, block):
        source = sources[head]
        rows = pl.ds(block * BLOCK, BLOCK)
        keep = 1.0 - meta[1 + seq * groups + block].astype(F32)
        own = source[rows, 0 : 4 * KEYS]
        if block == 0:
            before = edges[head][:, 0 : 4 * KEYS]
        else:
            before = source[pl.ds(block * BLOCK - 8, 8), 0 : 4 * KEYS]
        shifted, conv = convolve(own, before * keep, taps[head])
        sig = jax.nn.sigmoid(conv)
        active = conv * sig
        slope = sig * (1.0 + conv * (1.0 - sig))
        yield
        query_unit, query_inv = unit(active[:, :KEYS])
        query = query_unit * KEYS ** (-0.5)
        keys, keys_inv = unit(active[:, KEYS : 2 * KEYS])
        values = active[:, 2 * KEYS :]
        yield
        decay_pre, log_decay, strength, cumlog, ratio = decay_of(
            source[rows, 6 * KEYS : 6 * KEYS + 2], params[head, 0], params[head, 1], row, col
        )
        yield
        gamma = jnp.exp(cumlog)
        last = cumlog[BLOCK - 1 :]
        tail_scale = jnp.exp(last - cumlog)
        both = mm_nt(jnp.concatenate([keys, query], axis=0), keys)
        yield
        near = jnp.where(row > col, ratio * both[:BLOCK], 0.0)
        scores = both[BLOCK:] * ratio
        inverse = inverses[block, head]
        held = states[block, head]
        weight = mm(inverse, (strength * gamma) * keys).astype(LOW)
        key_state = mm(keys, held)
        yield
        lacking = values - gamma * key_state
        fresh = mm(inverse, strength * lacking)
        yield
        outcome = os[head][rows, :]
        d_mixed = dms[head][rows, :]
        gate = source[rows, 4 * KEYS : 6 * KEYS]
        gate_sig = jax.nn.sigmoid(gate)
        gate_act = gate * gate_sig
        inv = lax.rsqrt(jnp.mean(outcome * outcome, axis=1, keepdims=True) + 1e-06)
        normed = outcome * inv
        yield
        weighted = d_mixed * gain[...]
        d_gate = weighted * normed * (gate_sig * (1.0 + gate * (1.0 - gate_sig)))
        dsts[head][rows, 4 * KEYS : 6 * KEYS] = d_gate.astype(LOW)
        gain_parts.append(jnp.sum(d_mixed * normed * gate_act, axis=0, keepdims=True))
        yield
        d_normed = weighted * gate_act
        d_out = inv * (d_normed - normed * jnp.mean(d_normed * normed, axis=1, keepdims=True))
        d_out_low = d_out.astype(LOW)
        yield
        part_fresh = mm_tn(scores, d_out_low)
        part_state = mm_tn(query * gamma, d_out_low)
        tail = keys * tail_scale
        kept[block, head] = dict(
            keep=keep, shifted=shifted, slope=slope, query_unit=query_unit, query_inv=query_inv,
            query=query, keys=keys, keys_inv=keys_inv, decay_pre=decay_pre, log_decay=log_decay,
            strength=strength, ratio=ratio, gamma=gamma, last=jnp.exp(last), tail=tail,
            tail_scale=tail_scale, near=near, scores=scores, inverse=inverse, held=held,
            weight=weight, key_state=key_state, lacking=lacking, fresh=fresh,
            d_out_low=d_out_low, part_fresh=part_fresh, part_state=part_state,
        )

    side_by_side([recompute(head, block) for block, head in places], WIDTH)
    d_gain[...] += sum(gain_parts)
    current = [state_grad[0], state_grad[1]]
    for block in reversed(range(groups)):
        for head in range(2):
            k = kept[block, head]
            k["ds"] = current[head]
            d_fresh = (k["part_fresh"] + mm(k["tail"], current[head])).astype(LOW)
            k["d_fresh"] = d_fresh
            below = k["last"] * current[head] + k["part_state"] - mm_tn(k["weight"], d_fresh)
            current[head] = below * k["keep"]
    state_grad[0] = current[0]
    state_grad[1] = current[1]

    def differentiate(head, block):
        rows = pl.ds(block * BLOCK, BLOCK)
        k = kept[block, head]
        keys, query, gamma, strength = k["keys"], k["query"], k["gamma"], k["strength"]
        fresh_low = k["fresh"].astype(LOW)
        ds_low = k["ds"].astype(LOW)
        d_fill = mm_tn(k["inverse"], k["d_fresh"])
        yield
        grams = mm_nt(jnp.concatenate([d_fill.astype(LOW), k["d_out_low"]], axis=0), fresh_low)
        yield
        d_below = jnp.where(row > col, -grams[:BLOCK], 0.0)
        d_scores = grams[BLOCK:]
        d_tail = mm_nt(fresh_low, ds_low)
        scaled = (strength * gamma) * d_fill
        yield
        through = mm_nt(jnp.concatenate([k["d_out_low"], scaled.astype(LOW)], axis=0), k["held"])
        d_qk = (d_scores * k["ratio"]).astype(LOW)
        d_kk = (strength * d_below * k["ratio"]).astype(LOW)
        pair = mm(jnp.concatenate([d_qk, d_kk], axis=0), keys)
        yield
        d_query = gamma * through[:BLOCK] + pair[:BLOCK]
        d_keys = (
            pair[BLOCK:]
            - through[BLOCK:]
            + k["tail_scale"] * d_tail
            + mm_tn(jnp.concatenate([d_qk, d_kk], axis=0), jnp.concatenate([query, keys], axis=0))
        )
        yield
        d_values = strength * d_fill
        d_strength = rowsum(d_fill * k["lacking"]) + rowsum(d_below * k["near"])
        spread_grad = d_scores * k["scores"] + strength * d_below * k["near"]
        tail_part = rowsum(d_tail * k["tail"])
        d_cum = gamma * rowsum(query * through[:BLOCK]) - rowsum(scaled * k["key_state"]) - tail_part
        at_last = jnp.sum(tail_part, axis=0, keepdims=True) + k["last"] * jnp.sum(
            rowsum(k["ds"] * k["held"].astype(F32)), axis=0, keepdims=True
        )
        place = lax.broadcasted_iota(jnp.int32, (BLOCK, 1), 0)
        d_cum = d_cum + jnp.where(place == BLOCK - 1, at_last, 0.0)
        spread_grad = spread_grad + jnp.where(col == 0, d_cum, 0.0)
        yield
        d_log = rowsum(exact(lower, spread_grad, ((0,), (0,))) * after)
        d_log = d_log + jnp.where(place == 0, jnp.sum(d_cum, axis=0, keepdims=True), 0.0)
        yield
        d_decay = d_log * (-params[head, 0]) * jax.nn.sigmoid(k["decay_pre"])
        k["rate"] = jnp.sum(d_log * k["log_decay"], axis=0, keepdims=True)
        k["bias"] = jnp.sum(d_decay, axis=0, keepdims=True)
        d_write = d_strength * strength * (1.0 - strength)
        lanes = lax.broadcasted_iota(jnp.int32, (BLOCK, KEYS), 1)
        dsts[head][rows, 6 * KEYS : 7 * KEYS] = (
            jnp.where(lanes == 0, d_decay, 0.0) + jnp.where(lanes == 1, d_write, 0.0)
        ).astype(LOW)
        yield
        d_query = d_query * KEYS ** (-0.5)
        unit_q = k["query_unit"]
        d_active = jnp.concatenate(
            [
                k["query_inv"] * (d_query - unit_q * rowsum(unit_q * d_query)),
                k["keys_inv"] * (d_keys - keys * rowsum(keys * d_keys)),
                d_values,
            ],
            axis=1,
        )
        yield
        d_conv = d_active * k["slope"]
        k["d_conv"] = d_conv

    side_by_side([differentiate(head, block) for block, head in reversed(places)], WIDTH)
    for head in range(2):
        next_rows = carry[head]
        taps_here = taps[head]
        tap_sums = [jnp.zeros((1, 4 * KEYS), F32) for _ in range(4)]
        rate_sum = sum(kept[block, head]["rate"] for block in range(groups))
        bias_sum = sum(kept[block, head]["bias"] for block in range(groups))
        for block in reversed(range(groups)):
            rows = pl.ds(block * BLOCK, BLOCK)
            k = kept[block, head]
            d_conv = k["d_conv"]
            padded = jnp.concatenate([d_conv, next_rows], axis=0)
            d_own = taps_here[0:1] * d_conv
            tap_sums[0] = tap_sums[0] + jnp.sum(d_conv * k["shifted"][0], axis=0, keepdims=True)
            for lag in range(1, 4):
                moved = pltpu.roll(padded, BLOCK + 8 - lag, 0)[:BLOCK]
                d_own = d_own + taps_here[lag : lag + 1] * moved
                tap_sums[lag] = tap_sums[lag] + jnp.sum(
                    d_conv * k["shifted"][lag], axis=0, keepdims=True
                )
            dsts[head][rows, 0 : 4 * KEYS] = d_own.astype(LOW)
            next_rows = d_conv[0:8] * k["keep"]
        carry[head] = next_rows
        for lag in range(4):
            d_taps[head, lag : lag + 1, :] += tap_sums[lag]
        lane = lax.broadcasted_iota(jnp.int32, (1, KEYS), 1)
        d_params[head : head + 1, :] += jnp.where(lane == 0, rate_sum, 0.0) + jnp.where(
            lane == 1, bias_sum, 0.0
        )
    back = mm_nt(d_mine[...], mix_mine[:, : 7 * KEYS]) + mm_nt(d_other[...], mix_other[:, : 7 * KEYS])
    inward[...] = back.astype(LOW)
    d_norm_gain[...] += jnp.sum(back * normed_in[...].astype(F32), axis=0, keepdims=True)


def ffn_forward_kernel(rows, mine, other, u_a, u_b, act_a, act_b, out):
    half = mine.shape[1] // 3
    total = None
    for weight, u_out, act in ((mine, u_a, act_a), (other, u_b, act_b)):
        u = mm(rows[...], weight[:, : 2 * half])
        u_out[...] = u
        gate = u[:, :half]
        active = (gate * jax.nn.sigmoid(gate) * u[:, half:]).astype(LOW)
        act[...] = active
        piece = mm_nt(active, weight[:, 2 * half :])
        total = piece if total is None else total + piece
    out[...] = total.astype(LOW)


def ffn_backward_kernel(grad, u_a, u_b, mine, other, d_a, d_b, out):
    half = mine.shape[1] // 3
    total = None
    for weight, u_in, d_out in ((mine, u_a, d_a), (other, u_b, d_b)):
        d_active = mm(grad[...], weight[:, 2 * half :])
        gate, lift = u_in[:, :half], u_in[:, half:]
        sig = jax.nn.sigmoid(gate)
        d_gate = (d_active * lift * (sig * (1.0 + gate * (1.0 - sig)))).astype(LOW)
        d_lift = (d_active * (gate * sig)).astype(LOW)
        d_out[:, :half] = d_gate
        d_out[:, half:] = d_lift
        piece = mm_nt(d_gate, weight[:, :half]) + mm_nt(d_lift, weight[:, half : 2 * half])
        total = piece if total is None else total + piece
    out[...] = total.astype(LOW)


def ffn_forward(rows, weights):
    count, width = rows.shape
    half = weights[0].shape[1] // 3
    return pl.pallas_call(
        ffn_forward_kernel,
        out_shape=[
            jax.ShapeDtypeStruct((count, 2 * half), F32),
            jax.ShapeDtypeStruct((count, 2 * half), F32),
            jax.ShapeDtypeStruct((count, half), LOW),
            jax.ShapeDtypeStruct((count, half), LOW),
            jax.ShapeDtypeStruct((count, width), LOW),
        ],
        compiler_params=pltpu.CompilerParams(vmem_limit_bytes=FFN_VMEM),
        name="ffn_forward",
    )(rows, *weights)


def ffn_backward(grad, pair, weights):
    count, width = grad.shape
    half = weights[0].shape[1] // 3
    return pl.pallas_call(
        ffn_backward_kernel,
        out_shape=[
            jax.ShapeDtypeStruct((count, 2 * half), LOW),
            jax.ShapeDtypeStruct((count, 2 * half), LOW),
            jax.ShapeDtypeStruct((count, width), LOW),
        ],
        compiler_params=pltpu.CompilerParams(vmem_limit_bytes=FFN_VMEM),
        name="ffn_backward",
    )(grad, *pair, *weights)


def whole(array):
    return pl.BlockSpec(array.shape, lambda step, meta: (0,) * array.ndim)


def mixer_forward(meta, params, normed, weights, taps, gain, parts):
    rows, width = normed.shape
    wide = 7 * KEYS
    group = rows // parts
    per = group // BLOCK

    def place(step, meta):
        return (step ^ meta[0], 0)

    def stacked(step, meta):
        return (step, 0, 0, 0)

    vals = 2 * KEYS
    row_spec = pl.BlockSpec((group, vals), place)
    wide_spec = pl.BlockSpec((group, wide), place)
    full_spec = pl.BlockSpec((group, width), place)
    return pl.pallas_call(
        mixer_forward_kernel,
        grid_spec=pltpu.PrefetchScalarGridSpec(
            num_scalar_prefetch=1,
            grid=(parts,),
            in_specs=[
                pl.BlockSpec(memory_space=pltpu.SMEM),
                full_spec,
                *[whole(weight) for weight in weights],
                whole(taps),
                whole(gain),
            ],
            out_specs=[
                wide_spec,
                wide_spec,
                row_spec,
                row_spec,
                row_spec,
                row_spec,
                pl.BlockSpec((per, 2, KEYS, vals), stacked),
                pl.BlockSpec((per, 2, BLOCK, BLOCK), stacked),
                full_spec,
            ],
            scratch_shapes=[pltpu.VMEM((2, KEYS, vals), F32), pltpu.VMEM((2, 8, 4 * KEYS), F32)],
        ),
        out_shape=[
            jax.ShapeDtypeStruct((rows, wide), F32),
            jax.ShapeDtypeStruct((rows, wide), F32),
            jax.ShapeDtypeStruct((rows, vals), LOW),
            jax.ShapeDtypeStruct((rows, vals), LOW),
            jax.ShapeDtypeStruct((rows, vals), F32),
            jax.ShapeDtypeStruct((rows, vals), F32),
            jax.ShapeDtypeStruct((rows // BLOCK, 2, KEYS, vals), LOW),
            jax.ShapeDtypeStruct((rows // BLOCK, 2, BLOCK, BLOCK), LOW),
            jax.ShapeDtypeStruct((rows, width), LOW),
        ],
        compiler_params=pltpu.CompilerParams(vmem_limit_bytes=MIXER_VMEM),
        name="mixer_forward",
    )(meta, params, normed, *weights, taps, gain)


def mixer_backward(meta, params, saved, normed, d_branch, weights, taps, gain, parts):
    mine, other, o_a, o_b, states, inverses = saved
    rows, width = normed.shape
    wide = mine.shape[1]
    group = rows // parts
    per = group // BLOCK

    def place(step, meta):
        return ((parts - 1 - step) ^ meta[0], 0)

    def edge(step, meta):
        return ((jnp.maximum(parts - 2 - step, 0) ^ meta[0]) * (group // 8) + group // 8 - 1, 0)

    def stacked(step, meta):
        return (parts - 1 - step, 0, 0, 0)

    vals = 2 * KEYS
    row_spec = pl.BlockSpec((group, vals), place)
    wide_spec = pl.BlockSpec((group, wide), place)
    full_spec = pl.BlockSpec((group, width), place)
    edge_spec = pl.BlockSpec((8, wide), edge)
    return pl.pallas_call(
        mixer_backward_kernel,
        grid_spec=pltpu.PrefetchScalarGridSpec(
            num_scalar_prefetch=1,
            grid=(parts,),
            in_specs=[
                pl.BlockSpec(memory_space=pltpu.SMEM),
                wide_spec,
                wide_spec,
                edge_spec,
                edge_spec,
                row_spec,
                row_spec,
                full_spec,
                full_spec,
                pl.BlockSpec((per, 2, KEYS, vals), stacked),
                pl.BlockSpec((per, 2, BLOCK, BLOCK), stacked),
                *[whole(weight) for weight in weights],
                whole(taps),
                whole(gain),
            ],
            out_specs=[
                wide_spec,
                wide_spec,
                whole(taps),
                whole(gain),
                pl.BlockSpec((2, KEYS), lambda step, meta: (0, 0)),
                full_spec,
                pl.BlockSpec((1, width), lambda step, meta: (0, 0)),
            ],
            scratch_shapes=[
                pltpu.VMEM((2, KEYS, vals), F32),
                pltpu.VMEM((2, 8, 4 * KEYS), F32),
                pltpu.VMEM((group, vals), F32),
                pltpu.VMEM((group, vals), F32),
            ],
        ),
        out_shape=[
            jax.ShapeDtypeStruct((rows, wide), LOW),
            jax.ShapeDtypeStruct((rows, wide), LOW),
            jax.ShapeDtypeStruct(taps.shape, F32),
            jax.ShapeDtypeStruct(gain.shape, F32),
            jax.ShapeDtypeStruct((2, KEYS), F32),
            jax.ShapeDtypeStruct((rows, width), LOW),
            jax.ShapeDtypeStruct((1, width), F32),
        ],
        compiler_params=pltpu.CompilerParams(vmem_limit_bytes=MIXER_VMEM),
        name="mixer_backward",
    )(
        meta, params, mine, other, mine, other, o_a, o_b, normed, d_branch, states, inverses,
        *weights, taps, gain,
    )


def swap_section(array):
    return lax.ppermute(array, "section", [(0, 1), (1, 0)])


def send_by(array, offset):
    peers = lax.axis_size("tensor")
    return lax.ppermute(array, "tensor", [(i, i ^ offset) for i in range(peers)])


def spread_rows(values):
    peers = lax.axis_size("tensor")
    return [values] + [send_by(values, k) for k in range(1, peers)]


def collect_rows(parts):
    total = parts[0].astype(F32)
    for k in range(1, len(parts)):
        total = total + send_by(parts[k].astype(LOW), k).astype(F32)
    return total


def nn(left, right):
    return jnp.dot(left, right, preferred_element_type=F32)


def nt(left, right):
    return lax.dot_general(left, right, (((1,), (1,)), ((), ())), preferred_element_type=F32)


def tn(left, right):
    return lax.dot_general(left, right, (((0,), (0,)), ((), ())), preferred_element_type=F32)


def norm_forward(hidden, gain):
    inv = lax.rsqrt(jnp.mean(hidden * hidden, axis=-1, keepdims=True) + 1e-06)
    return (hidden * inv * gain).astype(LOW), inv


def norm_backward(hidden, inv, gain, grad):
    normed = hidden * inv
    weighted = grad * gain
    back = inv * (weighted - normed * jnp.mean(weighted * normed, axis=-1, keepdims=True))
    return back, jnp.sum(grad * normed, axis=0)


def layout(lengths_row, buffer):
    ends = jnp.cumsum(lengths_row, dtype=jnp.int32)
    token = jnp.arange(buffer, dtype=jnp.int32)
    start = jnp.max(jnp.where(ends[None, :] <= token[:, None], ends[None, :], 0), axis=1)
    live = (token < ends[-1]).astype(F32)
    reset = ((token - start)[::BLOCK] == 0).astype(jnp.int32)
    return live, reset


def split_rows(array, count):
    size = array.shape[0] // count
    return [array[k * size : (k + 1) * size] for k in range(count)]


def layer_forward(hidden, weights, gains, small, meta, live, between, last):
    mix_weights = weights
    params, taps, gain_out = small
    peers = lax.axis_size("tensor")
    normed, inv_one = norm_forward(hidden, gains[0])
    normed_all = jnp.concatenate(spread_rows(normed), axis=0)
    if last is not None:
        normed_all, last = lax.optimization_barrier((normed_all, last))
        last = spread_rows(last)
    mine, other, mixed_a, mixed_b, o_a, o_b, states, inverses, branch = mixer_forward(
        meta, params, normed_all, mix_weights, taps, gain_out, peers
    )
    if last is not None:
        branch, last = lax.optimization_barrier((branch, last))
    branch = collect_rows(split_rows(branch, peers))
    after = hidden + live * branch
    normed_two, inv_two = norm_forward(after, gains[1])
    ffn_weights = between(normed_two)
    normed_two_all = spread_rows(normed_two)
    ups, actives, ffn = [], [], []
    for place, chunk in enumerate(normed_two_all):
        if place:
            chunk, ffn[-1] = lax.optimization_barrier((chunk, ffn[-1]))
        u_a, u_b, act_a, act_b, partial = ffn_forward(chunk, ffn_weights)
        ups.append((u_a, u_b))
        actives.append((act_a, act_b))
        ffn.append(partial)
    kept = (
        hidden, inv_one, normed_all, mine, other, o_a, o_b, states, inverses, mixed_a, mixed_b,
        after, inv_two, normed_two_all, ups, actives,
    )
    return ffn, kept, last, (mix_weights, ffn_weights)


def finish_forward(after, live, ffn):
    return (after + live * collect_rows(ffn)).astype(LOW)


def share(mine, other):
    got = swap_section(other.astype(LOW))
    return (mine + got.astype(F32)).astype(LOW)


def scatter(total):
    return lax.psum_scatter(total, "dp", scatter_dimension=0, tiled=True)


def scatter_direct(total):
    peers = lax.axis_size("dp")
    me = lax.axis_index("dp")
    size = total.shape[0] // peers

    def part(owner):
        return lax.dynamic_slice_in_dim(total, owner * size, size, 0)

    result = part(me).astype(F32)
    for k in range(1, peers):
        sent = part((me + k) % peers)
        result = result + lax.ppermute(
            sent, "dp", [(i, (i + k) % peers) for i in range(peers)]
        ).astype(F32)
    return result.astype(LOW)


def exchange_sum(array, axis):
    peers = lax.axis_size(axis)
    offset = 1
    while offset < peers:
        array = array + lax.ppermute(array, axis, [(i, i ^ offset) for i in range(peers)])
        offset *= 2
    return array


def layer_backward(grad, kept, weights, gains, small, meta, live, ffn_grads, waiting, beside, final):
    mix_weights, ffn_weights = weights
    params, taps, gain_out = small
    (
        hidden, inv_one, normed_all, mine, other, o_a, o_b, states, inverses, mixed_a, mixed_b,
        after, inv_two, normed_two_all, ups, actives,
    ) = kept
    peers = lax.axis_size("tensor")
    if ffn_grads is None:
        ffn_grads = spread_rows((live * grad).astype(LOW))
    d_ups, back = ([], []), []
    for chunk, pair in zip(ffn_grads, ups):
        d_a, d_b, partial = ffn_backward(chunk, pair, ffn_weights)
        d_ups[0].append(d_a)
        d_ups[1].append(d_b)
        back.append(partial)
    back_two = collect_rows(back)
    two_all = jnp.concatenate(normed_two_all, axis=0)
    ffn_all = jnp.concatenate(ffn_grads, axis=0)
    ffn_parts = []
    for side in range(2):
        d_up_all = jnp.concatenate(d_ups[side], axis=0)
        active_all = jnp.concatenate([pair[side] for pair in actives], axis=0)
        ffn_parts.append((tn(two_all, d_up_all), tn(ffn_all, active_all)))
    ffn_total = share(*[jnp.concatenate(part, axis=1) for part in ffn_parts])
    back, gain_two_grad = norm_backward(after, inv_two, gains[1], back_two)
    grad_after = grad + back
    branch_all = jnp.concatenate(spread_rows((live * grad_after).astype(LOW)), axis=0)
    out_total = share(tn(branch_all, mixed_a), tn(branch_all, mixed_b))
    early = jnp.concatenate([ffn_total, out_total], axis=1)
    early, branch_all, waiting = lax.optimization_barrier((early, branch_all, waiting))
    early_owned = scatter(early)
    d_mine, d_other, d_taps, d_gain, d_params, inward, gain_one_grad = mixer_backward(
        meta, params, (mine, other, o_a, o_b, states, inverses), normed_all, branch_all,
        mix_weights, taps, gain_out, peers,
    )
    waiting = beside(waiting)
    inward, waiting = lax.optimization_barrier((inward, waiting))
    mix_total = share(tn(normed_all, d_mine[:, : 6 * KEYS]), tn(normed_all, d_other[:, : 6 * KEYS]))
    pairs = jnp.concatenate([d[:, 6 * KEYS : 6 * KEYS + 2] for d in (d_mine, d_other)], axis=1)
    decay_grad = tn(pairs, normed_all)
    gain_one_grad = gain_one_grad[0] / gains[0]
    small_grads = (jnp.stack([gain_one_grad, gain_two_grad]), d_taps, d_params, d_gain, decay_grad)
    early_owned, mix_total = lax.optimization_barrier((early_owned, mix_total))
    if final is not None:
        early_owned, mix_total, inward, small_grads = lax.optimization_barrier(
            (early_owned, mix_total, inward, small_grads)
        )
    if final is None:
        mix_owned = scatter(mix_total)
    else:
        (own, pairs), mix_total = lax.optimization_barrier((final(small_grads), mix_total))
        mix_owned = scatter_direct(mix_total)
        small_grads, inward = lax.optimization_barrier(
            ((exchange_sum(own, "tensor"), pairs), inward)
        )
    back_one = collect_rows(split_rows(inward, peers))
    back, _ = norm_backward(hidden, inv_one, gains[0], back_one)
    return (
        grad_after + back,
        [early_owned, mix_owned],
        small_grads,
        waiting,
    )


def on_device(
    inputs, lengths, norm_gain, w_query, w_key, w_value, w_gate, w_decay, conv_weight, head_rate,
    head_bias, out_gain, w_out, w_updown, w_down, cotangent,
):
    section = lax.axis_index("section")
    layers = lax.axis_size("section")
    first = section == 0
    part = lax.axis_index("tensor")
    rows_here = inputs.shape[1]
    buffer = rows_here * lax.axis_size("tensor")
    ff = w_down.shape[1]
    half = ff // 2
    wide = -(-half // KEYS) * KEYS
    vals = 2 * KEYS

    def zeros(count):
        return jnp.zeros((w_query.shape[1], count), LOW)

    def half_mix(h):
        return jnp.concatenate(
            [
                w_query[0][:, h * KEYS : (h + 1) * KEYS],
                w_key[0][:, h * KEYS : (h + 1) * KEYS],
                w_value[0][:, h * vals : (h + 1) * vals],
                w_gate[0][:, h * vals : (h + 1) * vals],
                w_decay[0][:, h * 2 : (h + 1) * 2],
                zeros(KEYS - 2),
                w_out[0][h * vals : (h + 1) * vals].T,
            ],
            axis=1,
        )

    def half_ffn(h):
        hidden_part = slice(h * half, (h + 1) * half)
        return jnp.concatenate(
            [
                w_updown[0][:, 0, hidden_part],
                zeros(wide - half),
                w_updown[0][:, 1, hidden_part],
                zeros(wide - half),
                w_down[0][hidden_part].T,
                zeros(wide - half),
            ],
            axis=1,
        )

    def both_layers(halves):
        keep = jnp.where(first, halves[0], halves[1])
        got = swap_section(jnp.where(first, halves[1], halves[0]))
        return jnp.where(first, keep, got), jnp.where(first, got, keep)

    mix_shards = both_layers((half_mix(0), half_mix(1)))
    ffn_shards = both_layers((half_ffn(0), half_ffn(1)))

    def gather(shard, *before):
        if before:
            shard, *before = lax.optimization_barrier((shard, *before))
        full = lax.all_gather(shard, "dp", axis=0, tiled=True)
        return (full, *before)

    def of_all(array):
        got = swap_section(array)
        return jnp.concatenate(
            [jnp.where(first, array, got), jnp.where(first, got, array)], axis=0
        )

    gains_all = of_all(norm_gain)
    sizes = (conv_weight.size, head_rate.size, head_bias.size, out_gain.size)
    packed = of_all(
        jnp.concatenate(
            [conv_weight.reshape(-1), head_rate.reshape(-1), head_bias.reshape(-1), out_gain.reshape(-1)]
        )[None]
    )
    edges = [0]
    for size in sizes:
        edges.append(edges[-1] + size)
    heads = conv_weight.shape[2]
    places = [part * 2 + section, part * 2 + 1 - section]
    smalls = []
    for layer in range(2):
        conv, rate, bias, gain_out = (packed[layer, a:b] for a, b in zip(edges[:-1], edges[1:]))
        conv = conv.reshape(conv_weight.shape[1:])
        taps = jnp.concatenate(
            [lax.dynamic_slice_in_dim(conv, p, 1, 1) for p in places], axis=1
        ).transpose(1, 0, 2)
        scale = jnp.stack([jnp.exp(rate), bias], axis=1)
        params = jnp.concatenate([lax.dynamic_slice_in_dim(scale, p, 1, 0) for p in places], axis=0)
        smalls.append((params, taps, gain_out[None]))

    lengths_row = lax.dynamic_index_in_dim(lengths[:, 0], section, 0, keepdims=False)
    live_all, reset = layout(lengths_row, buffer)
    live = lax.dynamic_slice_in_dim(live_all, part * rows_here, rows_here)[:, None]
    meta = jnp.concatenate([part[None].astype(jnp.int32), reset])

    def own_micro(array):
        return lax.dynamic_index_in_dim(array, section, 0, keepdims=False).astype(F32)

    hidden = own_micro(inputs)
    (mix_full,) = gather(mix_shards[0])
    ffn_full, mix_full = gather(ffn_shards[0], mix_full)
    mix_pair = (mix_full, swap_section(mix_full))
    held = {}

    def first_mixed(normed):
        held["mix"], full, _ = gather(mix_shards[1], ffn_full, normed)
        return full, swap_section(full)

    def second_mixed(normed):
        return held["ffn"], swap_section(held["ffn"])

    ffn, saved, _, weights_one = layer_forward(
        hidden, mix_pair, gains_all[0], smalls[0], meta, live, first_mixed, None
    )
    kept = [saved]
    hidden = finish_forward(saved[11], live, ffn)
    held["ffn"], held["mix"], _ = gather(ffn_shards[1], held["mix"], hidden)
    hidden = hidden.astype(F32)
    mix_pair = (held["mix"], swap_section(held["mix"]))
    ffn_last, saved, spread, weights_two = layer_forward(
        hidden, mix_pair, gains_all[1], smalls[1], meta, live, second_mixed,
        (live * own_micro(cotangent)).astype(LOW),
    )
    kept.append(saved)
    weights = [weights_one, weights_two]

    def sum_small(last):
        flat = []
        for gain_grads, d_taps, d_params, d_gain, _ in (last, small_grads[1]):
            conv_full = jnp.zeros(conv_weight.shape[1:], F32)
            pair_full = jnp.zeros((heads, 2), F32)
            for side, p in enumerate(places):
                conv_full = lax.dynamic_update_slice_in_dim(conv_full, d_taps[side][:, None, :], p, 1)
                pair_full = lax.dynamic_update_slice_in_dim(
                    pair_full, d_params[side : side + 1, :2], p, 0
                )
            flat.append(
                jnp.concatenate(
                    [
                        conv_full.reshape(-1), pair_full[:, 0], pair_full[:, 1], d_gain.reshape(-1),
                        gain_grads.reshape(-1),
                    ]
                )
            )
        pairs = jnp.stack([last[4], small_grads[1][4]])
        sent = jnp.concatenate([jnp.where(first, flat[1], flat[0]), pairs[:, 2:].reshape(-1)])
        kept_here = jnp.concatenate([jnp.where(first, flat[0], flat[1]), pairs[:, :2].reshape(-1)])
        total = exchange_sum(kept_here + swap_section(sent), "dp")
        size = flat[0].size
        return total[:size], total[size:]

    grad = own_micro(cotangent)
    owned, small_grads = [None, None], [None, None]
    for layer in (1, 0):
        waiting = ffn_last if layer == 1 else owned[1]
        grad, owned[layer], small_grads[layer], waiting = layer_backward(
            grad, kept[layer], weights[layer], gains_all[layer], smalls[layer], meta, live,
            spread if layer == 1 else None, waiting,
            (lambda parts: finish_forward(kept[1][11], live, parts)) if layer == 1 else (lambda x: x),
            sum_small if layer == 0 else None,
        )
        if layer == 0:
            owned[1] = waiting
        else:
            result_low = waiting
        grad_low = grad.astype(LOW)
        grad = grad_low.astype(F32)

    def own_halves(kind):
        keep = jnp.where(first, owned[0][kind], owned[1][kind])
        got = swap_section(jnp.where(first, owned[1][kind], owned[0][kind]))
        return (
            jnp.where(first, keep, got).astype(F32),
            jnp.where(first, got, keep).astype(F32),
        )

    def columns(pair, start, size):
        return jnp.concatenate([side[:, start : start + size] for side in pair], axis=1)

    early_pair = own_halves(0)
    grad_updown = jnp.stack([columns(early_pair, 0, half), columns(early_pair, wide, half)], axis=1)
    grad_down = columns(early_pair, 2 * wide, half).T
    grad_out = columns(early_pair, 3 * wide, vals).T
    own, pairs = small_grads[0]
    pairs = lax.dynamic_slice_in_dim(
        pairs.reshape(2, 2, -1), lax.axis_index("dp") * w_query.shape[1], w_query.shape[1], 2
    )
    mix_pair = own_halves(1)
    grad_query = columns(mix_pair, 0, KEYS)
    grad_key = columns(mix_pair, KEYS, KEYS)
    grad_value = columns(mix_pair, 2 * KEYS, vals)
    grad_gate = columns(mix_pair, vals + 2 * KEYS, vals)

    keep = jnp.where(first, pairs[0], pairs[1])
    got = swap_section(jnp.where(first, pairs[1], pairs[0]))
    grad_decay = jnp.concatenate([jnp.where(first, keep, got), jnp.where(first, got, keep)], axis=0).T

    pieces = [own[a:b] for a, b in zip(edges[:-1], edges[1:])]
    return (
        result_low[None],
        grad_low[None],
        own[edges[-1] :].reshape(norm_gain.shape),
        grad_query[None],
        grad_key[None],
        grad_value[None],
        grad_gate[None],
        grad_decay[None],
        pieces[0].reshape(conv_weight.shape),
        pieces[1].reshape(head_rate.shape),
        pieces[2].reshape(head_bias.shape),
        pieces[3].reshape(out_gain.shape),
        grad_out[None],
        grad_updown[None],
        grad_down[None],
    )


def solution(mesh):
    in_specs = (
        P(None, ("dp", "tensor"), None),
        P(None, "dp", None),
        P("section", None, None),
        P("section", "dp", "tensor"),
        P("section", "dp", "tensor"),
        P("section", "dp", "tensor"),
        P("section", "dp", "tensor"),
        P("section", "dp", "tensor"),
        P("section", None, None, None),
        P("section", None),
        P("section", None),
        P("section", None),
        P("section", "tensor", "dp"),
        P("section", "dp", None, "tensor"),
        P("section", "tensor", "dp"),
        P(None, ("dp", "tensor"), None),
    )
    out_specs = (
        P("section", ("dp", "tensor"), None),
        P("section", ("dp", "tensor"), None),
        P("section", None, None),
        P("section", "dp", "tensor"),
        P("section", "dp", "tensor"),
        P("section", "dp", "tensor"),
        P("section", "dp", "tensor"),
        P("section", "dp", "tensor"),
        P("section", None, None, None),
        P("section", None),
        P("section", None),
        P("section", None),
        P("section", "tensor", "dp"),
        P("section", "dp", None, "tensor"),
        P("section", "tensor", "dp"),
    )
    return jax.shard_map(
        on_device, mesh=mesh, in_specs=in_specs, out_specs=out_specs, check_vma=False
    )
```

```python
import jax
import jax.numpy as jnp
from jax import lax
from jax.experimental import pallas as pl
from jax.experimental.pallas import tpu as pltpu
from jax.sharding import PartitionSpec as P

KEYS = 128
BLOCK = 64
F32 = jnp.float32
LOW = jnp.bfloat16
WIDTH = 8
MIXER_VMEM = 56 * 1024 * 1024
FFN_VMEM = 14 * 1024 * 1024


def _dot(left, right, dims):
    return lax.dot_general(
        left.astype(LOW), right.astype(LOW), (dims, ((), ())), preferred_element_type=F32
    )


def mm(left, right):
    return _dot(left, right, ((1,), (0,)))


def mm_nt(left, right):
    return _dot(left, right, ((1,), (1,)))


def mm_tn(left, right):
    return _dot(left, right, ((0,), (0,)))


def exact(left, right, dims=((1,), (0,))):
    high = right.astype(LOW)
    rest = right - high.astype(F32)
    middle = rest.astype(LOW)
    low = rest - middle.astype(F32)
    return _dot(left, high, dims) + (_dot(left, middle, dims) + _dot(left, low, dims))


def mm_split(left, right):
    left_high = left.astype(LOW)
    right_high = right.astype(LOW)
    left_low = (left - left_high.astype(F32)).astype(LOW)
    right_low = (right - right_high.astype(F32)).astype(LOW)
    return mm(left_high, right_high) + (mm(left_high, right_low) + mm(left_low, right_high))


def grid_of(size):
    row = lax.broadcasted_iota(jnp.int32, (size, size), 0)
    col = lax.broadcasted_iota(jnp.int32, (size, size), 1)
    return row, col


def rowsum(array):
    return jnp.sum(array, axis=1, keepdims=True)


def side_by_side(steps, width):
    for first in range(0, len(steps), width):
        running = steps[first : first + width]
        while running:
            running = [step for step in running if next(step, running) is not running]


def unit_lower_inverses(belows, row, col):
    ones = jnp.where(row == col, 1.0, 0.0)
    near = row // 2 == col // 2
    inverses = [ones - jnp.where(near, below, 0.0) for below in belows]
    half = 2
    while half < BLOCK:
        span = 2 * half
        part = (row // span == col // span) & (row % span >= half) & (col % span < half)
        pieces = [mm_split(jnp.where(part, b, 0.0), i) for b, i in zip(belows, inverses)]
        inverses = [i - mm_split(i, p) for p, i in zip(pieces, inverses)]
        half = span
    return inverses


def convolve(own, before, taps):
    padded = jnp.concatenate([before, own], axis=0)
    shifted = [own]
    total = taps[0:1] * own
    for lag in range(1, taps.shape[0]):
        moved = pltpu.roll(padded, lag, 0)[8:]
        shifted.append(moved)
        total = total + taps[lag : lag + 1] * moved
    return shifted, total


def decay_of(pair, rate_exp, bias, row, col):
    shifted = pair[:, 0:1] + bias
    soft = jnp.maximum(shifted, 0.0) + jnp.log1p(jnp.exp(-jnp.abs(shifted)))
    log_decay = -rate_exp * soft
    strength = jax.nn.sigmoid(pair[:, 1:2])
    lower = jnp.where(row >= col, 1.0, 0.0)
    after = jnp.where(row > col, 1.0, 0.0)
    spread = exact(lower, log_decay * after)
    cumlog = spread[:, 0:1] + log_decay[0:1]
    ratio = jnp.where(row >= col, jnp.exp(spread), 0.0)
    return shifted, log_decay, strength, cumlog, ratio


def unit(array, scale=1.0):
    inv = lax.rsqrt(rowsum(array * array) + 1e-06)
    return array * inv, inv * scale


def mixer_forward_kernel(
    meta, params, normed, mix_mine, mix_other, taps, gain,
    mine, other, mixed_a, mixed_b, o_a, o_b, states, inverses, branch, state, carry,
):
    step = pl.program_id(0)
    groups = mine.shape[0] // BLOCK
    row, col = grid_of(BLOCK)

    @pl.when(step == 0)
    def _():
        state[...] = jnp.zeros_like(state)
        carry[...] = jnp.zeros_like(carry)

    mine[...] = mm(normed[...], mix_mine[:, : 7 * KEYS])
    other[...] = mm(normed[...], mix_other[:, : 7 * KEYS])
    sources = (mine, other)
    outs = (mixed_a, mixed_b)
    os = (o_a, o_b)
    prepared = {}

    def prepare(head, block):
        source = sources[head]
        rows = pl.ds(block * BLOCK, BLOCK)
        keep = 1.0 - meta[1 + step * groups + block].astype(F32)
        own = source[rows, 0 : 4 * KEYS]
        if block == 0:
            before = carry[head]
        else:
            before = source[pl.ds(block * BLOCK - 8, 8), 0 : 4 * KEYS]
        _, conv = convolve(own, before * keep, taps[head])
        active = conv * jax.nn.sigmoid(conv)
        yield
        query, _ = unit(active[:, :KEYS])
        query = query * KEYS ** (-0.5)
        keys, _ = unit(active[:, KEYS : 2 * KEYS])
        values = active[:, 2 * KEYS :]
        yield
        _, _, strength, cumlog, ratio = decay_of(
            source[rows, 6 * KEYS : 6 * KEYS + 2], params[head, 0], params[head, 1], row, col
        )
        yield
        gamma = jnp.exp(cumlog)
        last = cumlog[BLOCK - 1 :]
        both = mm_nt(jnp.concatenate([keys, query], axis=0), keys)
        yield
        below = jnp.where(row > col, strength * ratio * both[:BLOCK], 0.0)
        scores = (both[BLOCK:] * ratio).astype(LOW)
        tail = (keys * jnp.exp(last - cumlog)).astype(LOW)
        prepared[block, head] = (
            below,
            ((strength * gamma) * keys).astype(LOW),
            (strength * values).astype(LOW),
            scores,
            tail,
            (query * gamma).astype(LOW),
            jnp.exp(last),
            keep,
        )

    places = [(block, head) for block in range(groups) for head in range(2)]
    side_by_side([prepare(head, block) for block, head in places], WIDTH)
    for head in range(2):
        carry[head] = sources[head][pl.ds(groups * BLOCK - 8, 8), 0 : 4 * KEYS]
    order = list(prepared)
    solved = unit_lower_inverses([prepared[place][0] for place in order], row, col)
    for place, inverse in zip(order, solved):
        inverse_low = inverse.astype(LOW)
        inverses[place[0], place[1]] = inverse_low
        _, scaled_keys, scaled_values, *rest = prepared[place]
        weight = mm(inverse_low, scaled_keys).astype(LOW)
        prepared[place] = (weight, mm(inverse_low, scaled_values), *rest)
    current = [state[0], state[1]]
    for block in range(groups):
        for head in range(2):
            weight, update, scores, tail, query_low, last, keep = prepared[block, head]
            held = current[head] * keep
            held_low = held.astype(LOW)
            states[block, head] = held_low
            fresh = (update - mm(weight, held_low)).astype(LOW)
            current[head] = last * held + mm_tn(tail, fresh)
            rows = pl.ds(block * BLOCK, BLOCK)
            outcome = mm(query_low, held_low) + mm(scores, fresh)
            os[head][rows, :] = outcome
            inv = lax.rsqrt(jnp.mean(outcome * outcome, axis=1, keepdims=True) + 1e-06)
            gate = sources[head][rows, 4 * KEYS : 6 * KEYS]
            mixed = outcome * inv * gain[...] * (gate * jax.nn.sigmoid(gate))
            outs[head][rows, :] = mixed.astype(LOW)
    state[0] = current[0]
    state[1] = current[1]
    branch[...] = (
        mm_nt(mixed_a[...], mix_mine[:, 7 * KEYS :])
        + mm_nt(mixed_b[...], mix_other[:, 7 * KEYS :])
    ).astype(LOW)


def mixer_backward_kernel(
    meta, params, mine, other, edge_a, edge_b, o_a, o_b, normed_in, d_branch, states, inverses,
    mix_mine, mix_other, taps, gain,
    d_mine, d_other, d_taps, d_gain, d_params, inward, d_norm_gain, state_grad, carry, dm_a, dm_b,
):
    step = pl.program_id(0)
    seq = pl.num_programs(0) - 1 - step
    groups = mine.shape[0] // BLOCK
    row, col = grid_of(BLOCK)

    @pl.when(step == 0)
    def _():
        state_grad[...] = jnp.zeros_like(state_grad)
        carry[...] = jnp.zeros_like(carry)
        d_taps[...] = jnp.zeros_like(d_taps)
        d_gain[...] = jnp.zeros_like(d_gain)
        d_params[...] = jnp.zeros_like(d_params)
        d_norm_gain[...] = jnp.zeros_like(d_norm_gain)

    dm_a[...] = mm(d_branch[...], mix_mine[:, 7 * KEYS :])
    dm_b[...] = mm(d_branch[...], mix_other[:, 7 * KEYS :])

    sources = (mine, other)
    edges = (edge_a, edge_b)
    os = (o_a, o_b)
    dms = (dm_a, dm_b)
    dsts = (d_mine, d_other)
    lower = jnp.where(row >= col, 1.0, 0.0)
    after = jnp.where(row > col, 1.0, 0.0)
    kept = {}
    gain_parts = []
    places = [(block, head) for block in range(groups) for head in range(2)]

    def recompute(head, block):
        source = sources[head]
        rows = pl.ds(block * BLOCK, BLOCK)
        keep = 1.0 - meta[1 + seq * groups + block].astype(F32)
        own = source[rows, 0 : 4 * KEYS]
        if block == 0:
            before = edges[head][:, 0 : 4 * KEYS]
        else:
            before = source[pl.ds(block * BLOCK - 8, 8), 0 : 4 * KEYS]
        shifted, conv = convolve(own, before * keep, taps[head])
        sig = jax.nn.sigmoid(conv)
        active = conv * sig
        slope = sig * (1.0 + conv * (1.0 - sig))
        yield
        query_unit, query_inv = unit(active[:, :KEYS])
        query = query_unit * KEYS ** (-0.5)
        keys, keys_inv = unit(active[:, KEYS : 2 * KEYS])
        values = active[:, 2 * KEYS :]
        yield
        decay_pre, log_decay, strength, cumlog, ratio = decay_of(
            source[rows, 6 * KEYS : 6 * KEYS + 2], params[head, 0], params[head, 1], row, col
        )
        yield
        gamma = jnp.exp(cumlog)
        last = cumlog[BLOCK - 1 :]
        tail_scale = jnp.exp(last - cumlog)
        both = mm_nt(jnp.concatenate([keys, query], axis=0), keys)
        yield
        near = jnp.where(row > col, ratio * both[:BLOCK], 0.0)
        scores = both[BLOCK:] * ratio
        inverse = inverses[block, head]
        held = states[block, head]
        weight = mm(inverse, (strength * gamma) * keys).astype(LOW)
        key_state = mm(keys, held)
        yield
        lacking = values - gamma * key_state
        fresh = mm(inverse, strength * lacking)
        yield
        outcome = os[head][rows, :]
        d_mixed = dms[head][rows, :]
        gate = source[rows, 4 * KEYS : 6 * KEYS]
        gate_sig = jax.nn.sigmoid(gate)
        gate_act = gate * gate_sig
        inv = lax.rsqrt(jnp.mean(outcome * outcome, axis=1, keepdims=True) + 1e-06)
        normed = outcome * inv
        yield
        weighted = d_mixed * gain[...]
        d_gate = weighted * normed * (gate_sig * (1.0 + gate * (1.0 - gate_sig)))
        dsts[head][rows, 4 * KEYS : 6 * KEYS] = d_gate.astype(LOW)
        gain_parts.append(jnp.sum(d_mixed * normed * gate_act, axis=0, keepdims=True))
        yield
        d_normed = weighted * gate_act
        d_out = inv * (d_normed - normed * jnp.mean(d_normed * normed, axis=1, keepdims=True))
        d_out_low = d_out.astype(LOW)
        yield
        part_fresh = mm_tn(scores, d_out_low)
        part_state = mm_tn(query * gamma, d_out_low)
        tail = keys * tail_scale
        kept[block, head] = dict(
            keep=keep, shifted=shifted, slope=slope, query_unit=query_unit, query_inv=query_inv,
            query=query, keys=keys, keys_inv=keys_inv, decay_pre=decay_pre, log_decay=log_decay,
            strength=strength, ratio=ratio, gamma=gamma, last=jnp.exp(last), tail=tail,
            tail_scale=tail_scale, near=near, scores=scores, inverse=inverse, held=held,
            weight=weight, key_state=key_state, lacking=lacking, fresh=fresh,
            d_out_low=d_out_low, part_fresh=part_fresh, part_state=part_state,
        )

    side_by_side([recompute(head, block) for block, head in places], WIDTH)
    d_gain[...] += sum(gain_parts)
    current = [state_grad[0], state_grad[1]]
    for block in reversed(range(groups)):
        for head in range(2):
            k = kept[block, head]
            k["ds"] = current[head]
            d_fresh = (k["part_fresh"] + mm(k["tail"], current[head])).astype(LOW)
            k["d_fresh"] = d_fresh
            below = k["last"] * current[head] + k["part_state"] - mm_tn(k["weight"], d_fresh)
            current[head] = below * k["keep"]
    state_grad[0] = current[0]
    state_grad[1] = current[1]

    def differentiate(head, block):
        rows = pl.ds(block * BLOCK, BLOCK)
        k = kept[block, head]
        keys, query, gamma, strength = k["keys"], k["query"], k["gamma"], k["strength"]
        fresh_low = k["fresh"].astype(LOW)
        ds_low = k["ds"].astype(LOW)
        d_fill = mm_tn(k["inverse"], k["d_fresh"])
        yield
        grams = mm_nt(jnp.concatenate([d_fill.astype(LOW), k["d_out_low"]], axis=0), fresh_low)
        yield
        d_below = jnp.where(row > col, -grams[:BLOCK], 0.0)
        d_scores = grams[BLOCK:]
        d_tail = mm_nt(fresh_low, ds_low)
        scaled = (strength * gamma) * d_fill
        yield
        through = mm_nt(jnp.concatenate([k["d_out_low"], scaled.astype(LOW)], axis=0), k["held"])
        d_qk = (d_scores * k["ratio"]).astype(LOW)
        d_kk = (strength * d_below * k["ratio"]).astype(LOW)
        pair = mm(jnp.concatenate([d_qk, d_kk], axis=0), keys)
        yield
        d_query = gamma * through[:BLOCK] + pair[:BLOCK]
        d_keys = (
            pair[BLOCK:]
            - through[BLOCK:]
            + k["tail_scale"] * d_tail
            + mm_tn(jnp.concatenate([d_qk, d_kk], axis=0), jnp.concatenate([query, keys], axis=0))
        )
        yield
        d_values = strength * d_fill
        d_strength = rowsum(d_fill * k["lacking"]) + rowsum(d_below * k["near"])
        spread_grad = d_scores * k["scores"] + strength * d_below * k["near"]
        tail_part = rowsum(d_tail * k["tail"])
        d_cum = gamma * rowsum(query * through[:BLOCK]) - rowsum(scaled * k["key_state"]) - tail_part
        at_last = jnp.sum(tail_part, axis=0, keepdims=True) + k["last"] * jnp.sum(
            rowsum(k["ds"] * k["held"].astype(F32)), axis=0, keepdims=True
        )
        place = lax.broadcasted_iota(jnp.int32, (BLOCK, 1), 0)
        d_cum = d_cum + jnp.where(place == BLOCK - 1, at_last, 0.0)
        spread_grad = spread_grad + jnp.where(col == 0, d_cum, 0.0)
        yield
        d_log = rowsum(exact(lower, spread_grad, ((0,), (0,))) * after)
        d_log = d_log + jnp.where(place == 0, jnp.sum(d_cum, axis=0, keepdims=True), 0.0)
        yield
        d_decay = d_log * (-params[head, 0]) * jax.nn.sigmoid(k["decay_pre"])
        k["rate"] = jnp.sum(d_log * k["log_decay"], axis=0, keepdims=True)
        k["bias"] = jnp.sum(d_decay, axis=0, keepdims=True)
        d_write = d_strength * strength * (1.0 - strength)
        lanes = lax.broadcasted_iota(jnp.int32, (BLOCK, KEYS), 1)
        dsts[head][rows, 6 * KEYS : 7 * KEYS] = (
            jnp.where(lanes == 0, d_decay, 0.0) + jnp.where(lanes == 1, d_write, 0.0)
        ).astype(LOW)
        yield
        d_query = d_query * KEYS ** (-0.5)
        unit_q = k["query_unit"]
        d_active = jnp.concatenate(
            [
                k["query_inv"] * (d_query - unit_q * rowsum(unit_q * d_query)),
                k["keys_inv"] * (d_keys - keys * rowsum(keys * d_keys)),
                d_values,
            ],
            axis=1,
        )
        yield
        d_conv = d_active * k["slope"]
        k["d_conv"] = d_conv

    side_by_side([differentiate(head, block) for block, head in reversed(places)], WIDTH)
    for head in range(2):
        next_rows = carry[head]
        taps_here = taps[head]
        tap_sums = [jnp.zeros((1, 4 * KEYS), F32) for _ in range(4)]
        rate_sum = sum(kept[block, head]["rate"] for block in range(groups))
        bias_sum = sum(kept[block, head]["bias"] for block in range(groups))
        for block in reversed(range(groups)):
            rows = pl.ds(block * BLOCK, BLOCK)
            k = kept[block, head]
            d_conv = k["d_conv"]
            padded = jnp.concatenate([d_conv, next_rows], axis=0)
            d_own = taps_here[0:1] * d_conv
            tap_sums[0] = tap_sums[0] + jnp.sum(d_conv * k["shifted"][0], axis=0, keepdims=True)
            for lag in range(1, 4):
                moved = pltpu.roll(padded, BLOCK + 8 - lag, 0)[:BLOCK]
                d_own = d_own + taps_here[lag : lag + 1] * moved
                tap_sums[lag] = tap_sums[lag] + jnp.sum(
                    d_conv * k["shifted"][lag], axis=0, keepdims=True
                )
            dsts[head][rows, 0 : 4 * KEYS] = d_own.astype(LOW)
            next_rows = d_conv[0:8] * k["keep"]
        carry[head] = next_rows
        for lag in range(4):
            d_taps[head, lag : lag + 1, :] += tap_sums[lag]
        lane = lax.broadcasted_iota(jnp.int32, (1, KEYS), 1)
        d_params[head : head + 1, :] += jnp.where(lane == 0, rate_sum, 0.0) + jnp.where(
            lane == 1, bias_sum, 0.0
        )
    back = mm_nt(d_mine[...], mix_mine[:, : 7 * KEYS]) + mm_nt(d_other[...], mix_other[:, : 7 * KEYS])
    inward[...] = back.astype(LOW)
    d_norm_gain[...] += jnp.sum(back * normed_in[...].astype(F32), axis=0, keepdims=True)


def ffn_forward_kernel(rows, mine, other, u_a, u_b, act_a, act_b, out):
    half = mine.shape[1] // 3
    total = None
    for weight, u_out, act in ((mine, u_a, act_a), (other, u_b, act_b)):
        u = mm(rows[...], weight[:, : 2 * half])
        u_out[...] = u
        gate = u[:, :half]
        active = (gate * jax.nn.sigmoid(gate) * u[:, half:]).astype(LOW)
        act[...] = active
        piece = mm_nt(active, weight[:, 2 * half :])
        total = piece if total is None else total + piece
    out[...] = total.astype(LOW)


def ffn_backward_kernel(grad, u_a, u_b, mine, other, d_a, d_b, out):
    half = mine.shape[1] // 3
    total = None
    for weight, u_in, d_out in ((mine, u_a, d_a), (other, u_b, d_b)):
        d_active = mm(grad[...], weight[:, 2 * half :])
        gate, lift = u_in[:, :half], u_in[:, half:]
        sig = jax.nn.sigmoid(gate)
        d_gate = (d_active * lift * (sig * (1.0 + gate * (1.0 - sig)))).astype(LOW)
        d_lift = (d_active * (gate * sig)).astype(LOW)
        d_out[:, :half] = d_gate
        d_out[:, half:] = d_lift
        piece = mm_nt(d_gate, weight[:, :half]) + mm_nt(d_lift, weight[:, half : 2 * half])
        total = piece if total is None else total + piece
    out[...] = total.astype(LOW)


def ffn_forward(rows, weights):
    count, width = rows.shape
    half = weights[0].shape[1] // 3
    return pl.pallas_call(
        ffn_forward_kernel,
        out_shape=[
            jax.ShapeDtypeStruct((count, 2 * half), F32),
            jax.ShapeDtypeStruct((count, 2 * half), F32),
            jax.ShapeDtypeStruct((count, half), LOW),
            jax.ShapeDtypeStruct((count, half), LOW),
            jax.ShapeDtypeStruct((count, width), LOW),
        ],
        compiler_params=pltpu.CompilerParams(vmem_limit_bytes=FFN_VMEM),
        name="ffn_forward",
    )(rows, *weights)


def ffn_backward(grad, pair, weights):
    count, width = grad.shape
    half = weights[0].shape[1] // 3
    return pl.pallas_call(
        ffn_backward_kernel,
        out_shape=[
            jax.ShapeDtypeStruct((count, 2 * half), LOW),
            jax.ShapeDtypeStruct((count, 2 * half), LOW),
            jax.ShapeDtypeStruct((count, width), LOW),
        ],
        compiler_params=pltpu.CompilerParams(vmem_limit_bytes=FFN_VMEM),
        name="ffn_backward",
    )(grad, *pair, *weights)


def whole(array):
    return pl.BlockSpec(array.shape, lambda step, meta: (0,) * array.ndim)


def mixer_forward(meta, params, normed, weights, taps, gain, parts):
    rows, width = normed.shape
    wide = 7 * KEYS
    group = rows // parts
    per = group // BLOCK

    def place(step, meta):
        return (step ^ meta[0], 0)

    def stacked(step, meta):
        return (step, 0, 0, 0)

    vals = 2 * KEYS
    row_spec = pl.BlockSpec((group, vals), place)
    wide_spec = pl.BlockSpec((group, wide), place)
    full_spec = pl.BlockSpec((group, width), place)
    return pl.pallas_call(
        mixer_forward_kernel,
        grid_spec=pltpu.PrefetchScalarGridSpec(
            num_scalar_prefetch=1,
            grid=(parts,),
            in_specs=[
                pl.BlockSpec(memory_space=pltpu.SMEM),
                full_spec,
                *[whole(weight) for weight in weights],
                whole(taps),
                whole(gain),
            ],
            out_specs=[
                wide_spec,
                wide_spec,
                row_spec,
                row_spec,
                row_spec,
                row_spec,
                pl.BlockSpec((per, 2, KEYS, vals), stacked),
                pl.BlockSpec((per, 2, BLOCK, BLOCK), stacked),
                full_spec,
            ],
            scratch_shapes=[pltpu.VMEM((2, KEYS, vals), F32), pltpu.VMEM((2, 8, 4 * KEYS), F32)],
        ),
        out_shape=[
            jax.ShapeDtypeStruct((rows, wide), F32),
            jax.ShapeDtypeStruct((rows, wide), F32),
            jax.ShapeDtypeStruct((rows, vals), LOW),
            jax.ShapeDtypeStruct((rows, vals), LOW),
            jax.ShapeDtypeStruct((rows, vals), F32),
            jax.ShapeDtypeStruct((rows, vals), F32),
            jax.ShapeDtypeStruct((rows // BLOCK, 2, KEYS, vals), LOW),
            jax.ShapeDtypeStruct((rows // BLOCK, 2, BLOCK, BLOCK), LOW),
            jax.ShapeDtypeStruct((rows, width), LOW),
        ],
        compiler_params=pltpu.CompilerParams(vmem_limit_bytes=MIXER_VMEM),
        name="mixer_forward",
    )(meta, params, normed, *weights, taps, gain)


def mixer_backward(meta, params, saved, normed, d_branch, weights, taps, gain, parts):
    mine, other, o_a, o_b, states, inverses = saved
    rows, width = normed.shape
    wide = mine.shape[1]
    group = rows // parts
    per = group // BLOCK

    def place(step, meta):
        return ((parts - 1 - step) ^ meta[0], 0)

    def edge(step, meta):
        return ((jnp.maximum(parts - 2 - step, 0) ^ meta[0]) * (group // 8) + group // 8 - 1, 0)

    def stacked(step, meta):
        return (parts - 1 - step, 0, 0, 0)

    vals = 2 * KEYS
    row_spec = pl.BlockSpec((group, vals), place)
    wide_spec = pl.BlockSpec((group, wide), place)
    full_spec = pl.BlockSpec((group, width), place)
    edge_spec = pl.BlockSpec((8, wide), edge)
    return pl.pallas_call(
        mixer_backward_kernel,
        grid_spec=pltpu.PrefetchScalarGridSpec(
            num_scalar_prefetch=1,
            grid=(parts,),
            in_specs=[
                pl.BlockSpec(memory_space=pltpu.SMEM),
                wide_spec,
                wide_spec,
                edge_spec,
                edge_spec,
                row_spec,
                row_spec,
                full_spec,
                full_spec,
                pl.BlockSpec((per, 2, KEYS, vals), stacked),
                pl.BlockSpec((per, 2, BLOCK, BLOCK), stacked),
                *[whole(weight) for weight in weights],
                whole(taps),
                whole(gain),
            ],
            out_specs=[
                wide_spec,
                wide_spec,
                whole(taps),
                whole(gain),
                pl.BlockSpec((2, KEYS), lambda step, meta: (0, 0)),
                full_spec,
                pl.BlockSpec((1, width), lambda step, meta: (0, 0)),
            ],
            scratch_shapes=[
                pltpu.VMEM((2, KEYS, vals), F32),
                pltpu.VMEM((2, 8, 4 * KEYS), F32),
                pltpu.VMEM((group, vals), F32),
                pltpu.VMEM((group, vals), F32),
            ],
        ),
        out_shape=[
            jax.ShapeDtypeStruct((rows, wide), LOW),
            jax.ShapeDtypeStruct((rows, wide), LOW),
            jax.ShapeDtypeStruct(taps.shape, F32),
            jax.ShapeDtypeStruct(gain.shape, F32),
            jax.ShapeDtypeStruct((2, KEYS), F32),
            jax.ShapeDtypeStruct((rows, width), LOW),
            jax.ShapeDtypeStruct((1, width), F32),
        ],
        compiler_params=pltpu.CompilerParams(vmem_limit_bytes=MIXER_VMEM),
        name="mixer_backward",
    )(
        meta, params, mine, other, mine, other, o_a, o_b, normed, d_branch, states, inverses,
        *weights, taps, gain,
    )


def swap_section(array):
    return lax.ppermute(array, "section", [(0, 1), (1, 0)])


def send_by(array, offset):
    peers = lax.axis_size("tensor")
    return lax.ppermute(array, "tensor", [(i, i ^ offset) for i in range(peers)])


def spread_rows(values):
    peers = lax.axis_size("tensor")
    return [values] + [send_by(values, k) for k in range(1, peers)]


def collect_rows(parts):
    total = parts[0].astype(F32)
    for k in range(1, len(parts)):
        total = total + send_by(parts[k].astype(LOW), k).astype(F32)
    return total


def nn(left, right):
    return jnp.dot(left, right, preferred_element_type=F32)


def nt(left, right):
    return lax.dot_general(left, right, (((1,), (1,)), ((), ())), preferred_element_type=F32)


def tn(left, right):
    return lax.dot_general(left, right, (((0,), (0,)), ((), ())), preferred_element_type=F32)


def norm_forward(hidden, gain):
    inv = lax.rsqrt(jnp.mean(hidden * hidden, axis=-1, keepdims=True) + 1e-06)
    return (hidden * inv * gain).astype(LOW), inv


def norm_backward(hidden, inv, gain, grad):
    normed = hidden * inv
    weighted = grad * gain
    back = inv * (weighted - normed * jnp.mean(weighted * normed, axis=-1, keepdims=True))
    return back, jnp.sum(grad * normed, axis=0)


def layout(lengths_row, buffer):
    ends = jnp.cumsum(lengths_row, dtype=jnp.int32)
    token = jnp.arange(buffer, dtype=jnp.int32)
    start = jnp.max(jnp.where(ends[None, :] <= token[:, None], ends[None, :], 0), axis=1)
    live = (token < ends[-1]).astype(F32)
    reset = ((token - start)[::BLOCK] == 0).astype(jnp.int32)
    return live, reset


def split_rows(array, count):
    size = array.shape[0] // count
    return [array[k * size : (k + 1) * size] for k in range(count)]


def layer_forward(hidden, weights, gains, small, meta, live, between, last):
    mix_weights = weights
    params, taps, gain_out = small
    peers = lax.axis_size("tensor")
    normed, inv_one = norm_forward(hidden, gains[0])
    normed_all = jnp.concatenate(spread_rows(normed), axis=0)
    if last is not None:
        normed_all, last = lax.optimization_barrier((normed_all, last))
        last = spread_rows(last)
    mine, other, mixed_a, mixed_b, o_a, o_b, states, inverses, branch = mixer_forward(
        meta, params, normed_all, mix_weights, taps, gain_out, peers
    )
    if last is not None:
        branch, last = lax.optimization_barrier((branch, last))
    branch = collect_rows(split_rows(branch, peers))
    after = hidden + live * branch
    normed_two, inv_two = norm_forward(after, gains[1])
    ffn_weights = between(normed_two)
    normed_two_all = spread_rows(normed_two)
    ups, actives, ffn = [], [], []
    for place, chunk in enumerate(normed_two_all):
        if place:
            chunk, ffn[-1] = lax.optimization_barrier((chunk, ffn[-1]))
        u_a, u_b, act_a, act_b, partial = ffn_forward(chunk, ffn_weights)
        ups.append((u_a, u_b))
        actives.append((act_a, act_b))
        ffn.append(partial)
    kept = (
        hidden, inv_one, normed_all, mine, other, o_a, o_b, states, inverses, mixed_a, mixed_b,
        after, inv_two, normed_two_all, ups, actives,
    )
    return ffn, kept, last, (mix_weights, ffn_weights)


def finish_forward(after, live, ffn):
    return (after + live * collect_rows(ffn)).astype(LOW)


def share(mine, other):
    got = swap_section(other.astype(LOW))
    return (mine + got.astype(F32)).astype(LOW)


def scatter(total):
    return lax.psum_scatter(total, "dp", scatter_dimension=0, tiled=True)


def scatter_direct(total):
    peers = lax.axis_size("dp")
    me = lax.axis_index("dp")
    size = total.shape[0] // peers

    def part(owner):
        return lax.dynamic_slice_in_dim(total, owner * size, size, 0)

    result = part(me).astype(F32)
    for k in range(1, peers):
        sent = part((me + k) % peers)
        result = result + lax.ppermute(
            sent, "dp", [(i, (i + k) % peers) for i in range(peers)]
        ).astype(F32)
    return result.astype(LOW)


def exchange_sum(array, axis):
    peers = lax.axis_size(axis)
    offset = 1
    while offset < peers:
        array = array + lax.ppermute(array, axis, [(i, i ^ offset) for i in range(peers)])
        offset *= 2
    return array


def layer_backward(grad, kept, weights, gains, small, meta, live, ffn_grads, waiting, beside, final):
    mix_weights, ffn_weights = weights
    params, taps, gain_out = small
    (
        hidden, inv_one, normed_all, mine, other, o_a, o_b, states, inverses, mixed_a, mixed_b,
        after, inv_two, normed_two_all, ups, actives,
    ) = kept
    peers = lax.axis_size("tensor")
    if ffn_grads is None:
        ffn_grads = spread_rows((live * grad).astype(LOW))
    d_ups, back = ([], []), []
    for chunk, pair in zip(ffn_grads, ups):
        d_a, d_b, partial = ffn_backward(chunk, pair, ffn_weights)
        d_ups[0].append(d_a)
        d_ups[1].append(d_b)
        back.append(partial)
    back_two = collect_rows(back)
    two_all = jnp.concatenate(normed_two_all, axis=0)
    ffn_all = jnp.concatenate(ffn_grads, axis=0)
    ffn_parts = []
    for side in range(2):
        d_up_all = jnp.concatenate(d_ups[side], axis=0)
        active_all = jnp.concatenate([pair[side] for pair in actives], axis=0)
        ffn_parts.append((tn(two_all, d_up_all), tn(ffn_all, active_all)))
    ffn_total = share(*[jnp.concatenate(part, axis=1) for part in ffn_parts])
    back, gain_two_grad = norm_backward(after, inv_two, gains[1], back_two)
    grad_after = grad + back
    branch_all = jnp.concatenate(spread_rows((live * grad_after).astype(LOW)), axis=0)
    out_total = share(tn(branch_all, mixed_a), tn(branch_all, mixed_b))
    early = jnp.concatenate([ffn_total, out_total], axis=1)
    if final is None:
        branch_all, waiting = lax.optimization_barrier((branch_all, waiting))
    else:
        early, branch_all, waiting = lax.optimization_barrier((early, branch_all, waiting))
    early_owned = scatter(early)
    d_mine, d_other, d_taps, d_gain, d_params, inward, gain_one_grad = mixer_backward(
        meta, params, (mine, other, o_a, o_b, states, inverses), normed_all, branch_all,
        mix_weights, taps, gain_out, peers,
    )
    waiting = beside(waiting)
    inward, waiting = lax.optimization_barrier((inward, waiting))
    mix_total = share(tn(normed_all, d_mine[:, : 6 * KEYS]), tn(normed_all, d_other[:, : 6 * KEYS]))
    pairs = jnp.concatenate([d[:, 6 * KEYS : 6 * KEYS + 2] for d in (d_mine, d_other)], axis=1)
    decay_grad = tn(pairs, normed_all)
    gain_one_grad = gain_one_grad[0] / gains[0]
    small_grads = (jnp.stack([gain_one_grad, gain_two_grad]), d_taps, d_params, d_gain, decay_grad)
    early_owned, mix_total = lax.optimization_barrier((early_owned, mix_total))
    if final is not None:
        early_owned, mix_total, inward, small_grads = lax.optimization_barrier(
            (early_owned, mix_total, inward, small_grads)
        )
    if final is None:
        mix_owned = scatter(mix_total)
    else:
        (own, pairs), mix_total = lax.optimization_barrier((final(small_grads), mix_total))
        mix_owned = scatter_direct(mix_total)
        small_grads, inward = lax.optimization_barrier(
            ((exchange_sum(own, "tensor"), pairs), inward)
        )
    back_one = collect_rows(split_rows(inward, peers))
    back, _ = norm_backward(hidden, inv_one, gains[0], back_one)
    return (
        grad_after + back,
        [early_owned, mix_owned],
        small_grads,
        waiting,
    )


def on_device(
    inputs, lengths, norm_gain, w_query, w_key, w_value, w_gate, w_decay, conv_weight, head_rate,
    head_bias, out_gain, w_out, w_updown, w_down, cotangent,
):
    section = lax.axis_index("section")
    layers = lax.axis_size("section")
    first = section == 0
    part = lax.axis_index("tensor")
    rows_here = inputs.shape[1]
    buffer = rows_here * lax.axis_size("tensor")
    ff = w_down.shape[1]
    half = ff // 2
    wide = -(-half // KEYS) * KEYS
    vals = 2 * KEYS

    def zeros(count):
        return jnp.zeros((w_query.shape[1], count), LOW)

    def half_mix(h):
        return jnp.concatenate(
            [
                w_query[0][:, h * KEYS : (h + 1) * KEYS],
                w_key[0][:, h * KEYS : (h + 1) * KEYS],
                w_value[0][:, h * vals : (h + 1) * vals],
                w_gate[0][:, h * vals : (h + 1) * vals],
                w_decay[0][:, h * 2 : (h + 1) * 2],
                zeros(KEYS - 2),
                w_out[0][h * vals : (h + 1) * vals].T,
            ],
            axis=1,
        )

    def half_ffn(h):
        hidden_part = slice(h * half, (h + 1) * half)
        return jnp.concatenate(
            [
                w_updown[0][:, 0, hidden_part],
                zeros(wide - half),
                w_updown[0][:, 1, hidden_part],
                zeros(wide - half),
                w_down[0][hidden_part].T,
                zeros(wide - half),
            ],
            axis=1,
        )

    def both_layers(halves):
        keep = jnp.where(first, halves[0], halves[1])
        got = swap_section(jnp.where(first, halves[1], halves[0]))
        return jnp.where(first, keep, got), jnp.where(first, got, keep)

    mix_shards = both_layers((half_mix(0), half_mix(1)))
    ffn_shards = both_layers((half_ffn(0), half_ffn(1)))

    def gather(shard, *before):
        if before:
            shard, *before = lax.optimization_barrier((shard, *before))
        full = lax.all_gather(shard, "dp", axis=0, tiled=True)
        return (full, *before)

    def of_all(array):
        got = swap_section(array)
        return jnp.concatenate(
            [jnp.where(first, array, got), jnp.where(first, got, array)], axis=0
        )

    gains_all = of_all(norm_gain)
    sizes = (conv_weight.size, head_rate.size, head_bias.size, out_gain.size)
    packed = of_all(
        jnp.concatenate(
            [conv_weight.reshape(-1), head_rate.reshape(-1), head_bias.reshape(-1), out_gain.reshape(-1)]
        )[None]
    )
    edges = [0]
    for size in sizes:
        edges.append(edges[-1] + size)
    heads = conv_weight.shape[2]
    places = [part * 2 + section, part * 2 + 1 - section]
    smalls = []
    for layer in range(2):
        conv, rate, bias, gain_out = (packed[layer, a:b] for a, b in zip(edges[:-1], edges[1:]))
        conv = conv.reshape(conv_weight.shape[1:])
        taps = jnp.concatenate(
            [lax.dynamic_slice_in_dim(conv, p, 1, 1) for p in places], axis=1
        ).transpose(1, 0, 2)
        scale = jnp.stack([jnp.exp(rate), bias], axis=1)
        params = jnp.concatenate([lax.dynamic_slice_in_dim(scale, p, 1, 0) for p in places], axis=0)
        smalls.append((params, taps, gain_out[None]))

    lengths_row = lax.dynamic_index_in_dim(lengths[:, 0], section, 0, keepdims=False)
    live_all, reset = layout(lengths_row, buffer)
    live = lax.dynamic_slice_in_dim(live_all, part * rows_here, rows_here)[:, None]
    meta = jnp.concatenate([part[None].astype(jnp.int32), reset])

    def own_micro(array):
        return lax.dynamic_index_in_dim(array, section, 0, keepdims=False).astype(F32)

    hidden = own_micro(inputs)
    (mix_full,) = gather(mix_shards[0])
    ffn_full, mix_full = gather(ffn_shards[0], mix_full)
    mix_pair = (mix_full, swap_section(mix_full))
    held = {}

    def first_mixed(normed):
        held["mix"], full, _ = gather(mix_shards[1], ffn_full, normed)
        return full, swap_section(full)

    def second_mixed(normed):
        return held["ffn"], swap_section(held["ffn"])

    ffn, saved, _, weights_one = layer_forward(
        hidden, mix_pair, gains_all[0], smalls[0], meta, live, first_mixed, None
    )
    kept = [saved]
    hidden = finish_forward(saved[11], live, ffn)
    held["ffn"], held["mix"], _ = gather(ffn_shards[1], held["mix"], hidden)
    hidden = hidden.astype(F32)
    mix_pair = (held["mix"], swap_section(held["mix"]))
    ffn_last, saved, spread, weights_two = layer_forward(
        hidden, mix_pair, gains_all[1], smalls[1], meta, live, second_mixed,
        (live * own_micro(cotangent)).astype(LOW),
    )
    kept.append(saved)
    weights = [weights_one, weights_two]

    def sum_small(last):
        flat = []
        for gain_grads, d_taps, d_params, d_gain, _ in (last, small_grads[1]):
            conv_full = jnp.zeros(conv_weight.shape[1:], F32)
            pair_full = jnp.zeros((heads, 2), F32)
            for side, p in enumerate(places):
                conv_full = lax.dynamic_update_slice_in_dim(conv_full, d_taps[side][:, None, :], p, 1)
                pair_full = lax.dynamic_update_slice_in_dim(
                    pair_full, d_params[side : side + 1, :2], p, 0
                )
            flat.append(
                jnp.concatenate(
                    [
                        conv_full.reshape(-1), pair_full[:, 0], pair_full[:, 1], d_gain.reshape(-1),
                        gain_grads.reshape(-1),
                    ]
                )
            )
        pairs = jnp.stack([last[4], small_grads[1][4]])
        sent = jnp.concatenate([jnp.where(first, flat[1], flat[0]), pairs[:, 2:].reshape(-1)])
        kept_here = jnp.concatenate([jnp.where(first, flat[0], flat[1]), pairs[:, :2].reshape(-1)])
        total = exchange_sum(kept_here + swap_section(sent), "dp")
        size = flat[0].size
        return total[:size], total[size:]

    grad = own_micro(cotangent)
    owned, small_grads = [None, None], [None, None]
    for layer in (1, 0):
        waiting = ffn_last if layer == 1 else owned[1]
        grad, owned[layer], small_grads[layer], waiting = layer_backward(
            grad, kept[layer], weights[layer], gains_all[layer], smalls[layer], meta, live,
            spread if layer == 1 else None, waiting,
            (lambda parts: finish_forward(kept[1][11], live, parts)) if layer == 1 else (lambda x: x),
            sum_small if layer == 0 else None,
        )
        if layer == 0:
            owned[1] = waiting
        else:
            result_low = waiting
        grad_low = grad.astype(LOW)
        grad = grad_low.astype(F32)

    def own_halves(kind):
        keep = jnp.where(first, owned[0][kind], owned[1][kind])
        got = swap_section(jnp.where(first, owned[1][kind], owned[0][kind]))
        return (
            jnp.where(first, keep, got).astype(F32),
            jnp.where(first, got, keep).astype(F32),
        )

    def columns(pair, start, size):
        return jnp.concatenate([side[:, start : start + size] for side in pair], axis=1)

    early_pair = own_halves(0)
    grad_updown = jnp.stack([columns(early_pair, 0, half), columns(early_pair, wide, half)], axis=1)
    grad_down = columns(early_pair, 2 * wide, half).T
    grad_out = columns(early_pair, 3 * wide, vals).T
    own, pairs = small_grads[0]
    pairs = lax.dynamic_slice_in_dim(
        pairs.reshape(2, 2, -1), lax.axis_index("dp") * w_query.shape[1], w_query.shape[1], 2
    )
    mix_pair = own_halves(1)
    grad_query = columns(mix_pair, 0, KEYS)
    grad_key = columns(mix_pair, KEYS, KEYS)
    grad_value = columns(mix_pair, 2 * KEYS, vals)
    grad_gate = columns(mix_pair, vals + 2 * KEYS, vals)

    keep = jnp.where(first, pairs[0], pairs[1])
    got = swap_section(jnp.where(first, pairs[1], pairs[0]))
    grad_decay = jnp.concatenate([jnp.where(first, keep, got), jnp.where(first, got, keep)], axis=0).T

    pieces = [own[a:b] for a, b in zip(edges[:-1], edges[1:])]
    return (
        result_low[None],
        grad_low[None],
        own[edges[-1] :].reshape(norm_gain.shape),
        grad_query[None],
        grad_key[None],
        grad_value[None],
        grad_gate[None],
        grad_decay[None],
        pieces[0].reshape(conv_weight.shape),
        pieces[1].reshape(head_rate.shape),
        pieces[2].reshape(head_bias.shape),
        pieces[3].reshape(out_gain.shape),
        grad_out[None],
        grad_updown[None],
        grad_down[None],
    )


def solution(mesh):
    in_specs = (
        P(None, ("dp", "tensor"), None),
        P(None, "dp", None),
        P("section", None, None),
        P("section", "dp", "tensor"),
        P("section", "dp", "tensor"),
        P("section", "dp", "tensor"),
        P("section", "dp", "tensor"),
        P("section", "dp", "tensor"),
        P("section", None, None, None),
        P("section", None),
        P("section", None),
        P("section", None),
        P("section", "tensor", "dp"),
        P("section", "dp", None, "tensor"),
        P("section", "tensor", "dp"),
        P(None, ("dp", "tensor"), None),
    )
    out_specs = (
        P("section", ("dp", "tensor"), None),
        P("section", ("dp", "tensor"), None),
        P("section", None, None),
        P("section", "dp", "tensor"),
        P("section", "dp", "tensor"),
        P("section", "dp", "tensor"),
        P("section", "dp", "tensor"),
        P("section", "dp", "tensor"),
        P("section", None, None, None),
        P("section", None),
        P("section", None),
        P("section", None),
        P("section", "tensor", "dp"),
        P("section", "dp", None, "tensor"),
        P("section", "tensor", "dp"),
    )
    return jax.shard_map(
        on_device, mesh=mesh, in_specs=in_specs, out_specs=out_specs, check_vma=False
    )
```
